512 devices in a mesh: rep: 32 (over z, y_lo), shard: 16 (over y_hi, x, core).
Axes of the slice: x: 4, y: 8 (y_hi: 2, y_lo: 4; y = y_hi * 4 + y_lo), z: 8, core: 2. Of those that a mesh axis runs over, the one named last changes fastest.
Arguments:
- layer_inputs: bfloat16 [8192, 3072], P('rep', 'shard'), may hold values from -42 to 42
- output_cotangents: bfloat16 [8192, 3072], P('rep', 'shard'), may hold values from -42 to 42
- valid: int32 [8192], P('rep'), may hold values from 0 to 1, as said below
- factor_a_old: float32 [3072, 3072], P('rep', 'shard'), may hold values from -0.6 to 2.5
- factor_g_old: float32 [3072, 3072], P('rep', 'shard'), may hold values from -0.6 to 2.5
- weight_gradient: bfloat16 [3072, 3072], P('shard', 'rep'), may hold values from -0.59765625 to 0.59765625
- basis_g: bfloat16 [3072, 3072], P('shard'), may hold values from -0.109375 to 0.109375
- basis_a: bfloat16 [3072, 3072], P('shard', 'rep'), may hold values from -0.109375 to 0.109375
- spectrum_g: float32 [3072], replicated, may hold values from 0.1 to 1
- spectrum_a: float32 [3072], P('rep'), may hold values from 0.1 to 1
Outputs:
- factor_a_new: float32 [3072, 3072], P('rep', 'shard')
- factor_g_new: float32 [3072, 3072], P('rep', 'shard')
- preconditioned: bfloat16 [3072, 3072], P('shard')
The draws below stay inside these ranges and needn't reach their ends.
Inputs may be any that keep to these rules, and one draw needn't show every extreme that they name: The first token of every replica has valid = 1.
All inputs are finite; a program needn't handle non-finite values.
Results may differ from the reference program's by a relative error of at most 0.0095.
Values may be sent and summed in bfloat16 or wider, within the bound.
A program may use at most 64 MiB of HBM per device.

```python
import math
import jax
import jax.numpy as jnp
from jax import lax

W = 3072
TOK_REP = 256
TOKENS = 8192
N_REP = 32


def mixed_tokens(key, jitter):
    feature_key, block_key = jax.random.split(key, 2)
    feature_order = jax.random.permutation(feature_key, W)
    block_order = jax.random.permutation(block_key, N_REP)
    replica = jnp.arange(TOKENS, dtype=jnp.int32) // TOK_REP
    feature_block = jnp.arange(W, dtype=jnp.int32) // (W // N_REP)
    boosted = block_order[replica][:, None] == feature_block[None, :]
    mixed = jitter + 0.7 * jnp.take(jitter, feature_order, axis=1)
    values = mixed * jnp.where(boosted, 4.0, 1.0)
    return values.astype(jnp.bfloat16)


def draw_layer_inputs(key, part):
    key = jax.random.fold_in(key, 21)
    jitter_key = jax.random.fold_in(key, 5)
    jitter = jax.random.truncated_normal(jitter_key, -6.0, 6.0, (TOKENS, W), jnp.float32)
    return mixed_tokens(key, jitter)


def draw_output_cotangents(key, part):
    key = jax.random.fold_in(key, 22)
    jitter_key = jax.random.fold_in(key, 5)
    jitter = jax.random.truncated_normal(jitter_key, -6.0, 6.0, (TOKENS, W), jnp.float32)
    return mixed_tokens(key, jitter)


def running_factor(key):
    diagonal_key, jitter_key = jax.random.split(key, 2)
    diagonal = jnp.exp(jax.random.uniform(diagonal_key, (W,), jnp.float32, math.log(0.75), math.log(2.5)))
    jitter = 0.05 * jax.random.truncated_normal(jitter_key, -6.0, 6.0, (W, W), jnp.float32)
    symmetric = jitter + jitter.T
    indices = jnp.arange(W, dtype=jnp.int32)
    return jnp.where(indices[:, None] == indices[None, :], diagonal[None, :], symmetric).astype(jnp.float32)


def draw_factor_a_old(key, part):
    key = jax.random.fold_in(key, 31)
    return running_factor(key)


def draw_factor_g_old(key, part):
    key = jax.random.fold_in(key, 32)
    return running_factor(key)


def draw_valid(key, part):
    key = jax.random.fold_in(key, 11)
    positions = jnp.arange(TOKENS, dtype=jnp.int32)
    replica = positions // TOK_REP
    highest = max(TOKENS // TOK_REP - 1, 1)
    percent = 25 + 50 * replica // highest
    rolls = jax.random.randint(key, (TOKENS,), 0, 100, dtype=jnp.int32)
    chosen = (rolls < percent).astype(jnp.int32)
    return jnp.where(positions % TOK_REP == 0, 1, chosen).astype(jnp.int32)


def levels(stream_key, shape, cuts, low, largest):
    def one(dim, shards_of):
        heights = jax.random.uniform(jax.random.fold_in(jax.random.fold_in(stream_key, 6), dim), (shards_of,), jnp.float32, low / len(cuts), largest / len(cuts))
        return jnp.repeat(jnp.exp(heights), shape[dim] // shards_of).reshape((-1,) + (1,) * (len(shape) - dim - 1))

    gain = one(*cuts[0])
    for cut in cuts[1:]:
        gain = gain * one(*cut)
    return gain


def scatter_about(key, shape, width, bound, cuts=(), held_as=jnp.bfloat16):
    values = jax.random.normal(key, shape, jnp.float32) * width
    if len(cuts) > 0:
        values = levels(key, shape, cuts, -0.22, 0.18) * values
    return jnp.clip(values, min=-bound, max=bound).astype(held_as)


def setup_inputs(seed: int = 0) -> dict:
    seeds = jax.random.split(jax.random.key(seed), 11)
    layer_inputs = draw_layer_inputs(jax.random.fold_in(seeds[10], 71), 0)
    output_cotangents = draw_output_cotangents(jax.random.fold_in(seeds[10], 71), 0)
    valid = draw_valid(jax.random.fold_in(seeds[10], 71), 0)
    factor_a_old = draw_factor_a_old(jax.random.fold_in(seeds[10], 71), 0)
    factor_g_old = draw_factor_g_old(jax.random.fold_in(seeds[10], 71), 0)
    weight_gradient = scatter_about(seeds[5], (W, W), 0.1, 0.59765625, ((0, 16), (1, 32)))
    basis_g = scatter_about(seeds[6], (W, W), W ** -0.5, 0.109375, ((0, 16),))
    basis_a = scatter_about(seeds[7], (W, W), W ** -0.5, 0.109375, ((0, 16), (1, 32)))
    spectrum_g = jnp.clip(jnp.exp(jax.random.uniform(seeds[8], (W,), jnp.float32, math.log(0.1), math.log(1.0))), 0.1, 1.0)
    spectrum_a = jnp.clip(jnp.exp(math.log(1.0) - 2.3025851 * jax.random.uniform(seeds[9], (W,), jnp.float32) ** levels(seeds[9], (W,), ((0, 32),), -0.2, 0.2)), 0.1, 1.0)
    return dict(layer_inputs=layer_inputs, output_cotangents=output_cotangents, valid=valid, factor_a_old=factor_a_old, factor_g_old=factor_g_old, weight_gradient=weight_gradient, basis_g=basis_g, basis_a=basis_a, spectrum_g=spectrum_g, spectrum_a=spectrum_a)


DAMPING = 0.03
DECAY = 0.95


def reference(layer_inputs, output_cotangents, valid, factor_a_old, factor_g_old, weight_gradient, basis_g, basis_a, spectrum_g, spectrum_a):
    weights = valid.astype(jnp.bfloat16)
    count = jnp.sum(valid).astype(jnp.float32)
    input_blocks = layer_inputs.reshape(N_REP, TOK_REP, W)
    output_blocks = output_cotangents.reshape(N_REP, TOK_REP, W)
    mask_blocks = weights.reshape(N_REP, TOK_REP, 1)

    def add_replica(totals, block):
        input_block, output_block, mask_block = block
        stat_a = jnp.dot((input_block * mask_block).T, input_block, preferred_element_type=jnp.float32)
        stat_g = jnp.dot((output_block * mask_block).T, output_block, preferred_element_type=jnp.float32)
        stat_a = lax.optimization_barrier(stat_a.astype(jnp.bfloat16)).astype(jnp.float32)
        stat_g = lax.optimization_barrier(stat_g.astype(jnp.bfloat16)).astype(jnp.float32)
        return (totals[0] + stat_a, totals[1] + stat_g), jnp.zeros((), jnp.float32)

    empty = jnp.zeros((W, W), jnp.float32)
    summed, unused = lax.scan(add_replica, (empty, empty), (input_blocks, output_blocks, mask_blocks))
    scale = (1.0 - DECAY) / count
    factor_a_new = DECAY * factor_a_old + summed[0] * scale
    factor_g_new = DECAY * factor_g_old + summed[1] * scale

    rotated_in = jnp.dot(weight_gradient, basis_a, preferred_element_type=jnp.float32).astype(jnp.bfloat16)
    rotated = jnp.dot(basis_g.T, rotated_in, preferred_element_type=jnp.float32)
    scaled = (rotated / (spectrum_g[:, None] * spectrum_a[None, :] + DAMPING)).astype(jnp.bfloat16)
    back_out = jnp.dot(basis_g, scaled, preferred_element_type=jnp.float32).astype(jnp.bfloat16)
    preconditioned = jnp.dot(back_out, basis_a.T, preferred_element_type=jnp.float32).astype(jnp.bfloat16)
    return (factor_a_new, factor_g_new, preconditioned)
```

```python
import jax
import jax.numpy as jnp
from jax import lax
from jax.experimental import pallas as pl
from jax.experimental.pallas import tpu as pltpu
from jax.sharding import PartitionSpec as P

DAMPING = 0.03
DECAY = 0.95

NZ, NY, NQ, NX = 8, 4, 8, 4
BF, F32 = jnp.bfloat16, jnp.float32
NT = (((1,), (1,)), ((), ()))
TN = (((0,), (0,)), ((), ()))


def dot(a, b, dims=(((1,), (0,)), ((), ()))):
    return lax.dot_general(a, b, dims, preferred_element_type=F32)


def lanes4(parts):
    return jnp.concatenate([p.astype(F32) for p in parts], axis=1).astype(BF)


def kernel(
    xa, xg, mask, fa_old, fg_old, grad, bg, ba, sg, sa,
    fa_new, fg_new, out,
    d_buf, r_buf, c_buf, bap, az_s, az, cnt_y, cnt_s, cnt_z,
    gy, gfull, bcols, pt, half_s, half_r, keep, rs_s, rs_r, sc,
    boy, pz_s, pz, py,
    gy_ss, gy_rs, ring_ss, ring_rs, b_ss, b_rs, bf_ss, bf_rs,
    r1_ss, r2_ss, r3_ss, r_rs, c_ss, c_rs, n_ss, n_rs, m_ss, m_rs,
    h_ss, h_rs, p_ss, p_rs, s_ss, s_rs, sf_ss, sf_rs,
    a_ss, a_rs, o_ss, o_rs, z_ss, z_rs, q_ss, q_rs,
):
    r = lax.axis_index("rep")
    s = lax.axis_index("shard")
    z, y = lax.div(r, NY), lax.rem(r, NY)
    q, c = lax.div(s, 2), lax.rem(s, 2)
    yh, x = lax.div(q, NX), lax.rem(q, NX)
    half = lax.div(y, 2)

    def y_of(k):
        return lax.rem(y + k, NY)

    def z_of(k):
        return lax.rem(z + k, NZ)

    def q_of(k):
        return lax.rem(q + k, NQ)

    def y_dev(k):
        return (z * NY + y_of(k), s)

    def z_dev(k):
        return (z_of(k) * NY + y, s)

    def q_dev(k):
        return (r, q_of(k) * 2 + c)

    def x_dev(k):
        return (r, (yh * NX + lax.rem(x + k, NX)) * 2 + c)

    sib = (r, q * 2 + 1 - c)

    def far(src, dst, ss, rs, dev):
        return pltpu.make_async_remote_copy(
            src_ref=src, dst_ref=dst, send_sem=ss, recv_sem=rs,
            device_id=dev, device_id_type=pl.DeviceIdType.MESH,
        )

    def each(n, first=1):
        def deco(body):
            def step(k, carry):
                body(k)
                return carry
            lax.fori_loop(first, n, step, 0)
        return deco

    gate = pltpu.get_barrier_semaphore()

    def greet(dev):
        pl.semaphore_signal(gate, inc=1, device_id=dev, device_id_type=pl.DeviceIdType.MESH)

    each(NY)(lambda k: greet(y_dev(k)))
    each(NZ)(lambda k: greet(z_dev(k)))
    each(NQ)(lambda k: greet(q_dev(k)))
    greet(sib)
    own_piece = jnp.logical_and(half == c, yh == c)

    @each(NY, 0)
    def _(j):
        itself = jnp.logical_and(own_piece, j == y)

        @pl.when(jnp.logical_not(itself))
        def _():
            greet((z * NY + j, (c * NX + x) * 2 + half))

    pl.semaphore_wait(gate, 3 + 7 + 7 + 1 + 4 - jnp.where(own_piece, 1, 0))

    @each(NY)
    def _(k):
        far(grad, gy.at[y], gy_ss.at[k], gy_rs.at[k], y_dev(k)).start()

    b_own = bcols.at[pl.ds(pl.multiple_of(s * 192, 64), 192), :]

    @each(NQ)
    def _(k):
        far(ba, b_own, b_ss.at[k], b_rs.at[k], q_dev(k)).start()

    far(ba, b_own, bf_ss.at[0], bf_rs.at[0], sib).start()

    m = mask[...].astype(F32)
    d_buf[:, 0:256] = xa[...]
    d_buf[:, 256:512] = xg[...]
    d_buf[:, 512:640] = jnp.concatenate(
        [ba[...].astype(F32), jnp.zeros((192, 32), F32)], axis=1
    ).astype(BF)

    def piece(h, t):
        dev = (z * NY + 2 * c + h, (t * NX + x) * 2 + yh)
        itself = jnp.logical_and(dev[0] == r, dev[1] == s)
        src = d_buf.at[pl.ds(96 * h, 96), :]
        dst = r_buf.at[y, q]
        return itself, src, dst, far(src, dst, r1_ss.at[2 * h + t], r_rs.at[y, q], dev)

    for h in range(2):
        for t in range(2):
            itself, src, dst, copy = piece(h, t)

            @pl.when(jnp.logical_not(itself))
            def _():
                copy.start()

            @pl.when(itself)
            def _():
                pltpu.make_async_copy(src, dst, r_rs.at[y, q]).start()

    c_own = c_buf.at[y]
    c_own[:, 0:256] = (xa[...].astype(F32) * m).astype(BF)
    c_own[:, 256:512] = (xg[...].astype(F32) * m).astype(BF)
    cnt_y[y] = jnp.broadcast_to(jnp.sum(m, axis=1, keepdims=True), (8, 128))

    @each(NY)
    def _(k):
        far(c_own, c_own, c_ss.at[k], c_rs.at[k], y_dev(k)).start()
        far(cnt_y.at[y], cnt_y.at[y], n_ss.at[k], n_rs.at[k], y_dev(k)).start()

    b_own[...] = ba[...]

    def gather(own, four, full, y_ss, y_rs, ring, between):
        @each(NY)
        def _(k):
            slot = four.at[y_of(NY - k)]
            far(own, slot, y_ss.at[k], y_rs.at[k], y_dev(k)).wait_recv()

        four[y] = own[...]

        def at(zz, rows=pl.ds(0, 192)):
            return full.at[rows, pl.ds(pl.multiple_of(zz * 384, 128), 384)]

        at(z)[...] = lanes4([four[i] for i in range(NY)])
        for k in range(4):
            rows = [pl.ds(0, 192), pl.ds(0, 192)] if k < 3 else [pl.ds(0, 96), pl.ds(96, 96)]
            copies = []
            for way, sign in ((0, NZ - 1), (1, 1)):
                slot = at(z_of(sign * k), rows[way])
                came = at(z_of(sign * (k + 1)), rows[way])
                go = far(slot, slot, ring_ss.at[ring, way, k], ring_rs.at[ring, way, k],
                         z_dev(1 if way == 0 else NZ - 1))
                go.start()
                copies.append((go, far(came, came, ring_ss.at[ring, way, k], ring_rs.at[ring, way, k],
                                       z_dev(1 if way == 0 else NZ - 1))))
            between(k)
            for go, come in copies:
                come.wait_recv()

    def during_first(k):
        slot = r_buf.at[k, c * NX + x]
        far(slot, slot, r2_ss.at[0, k], r_rs.at[k, c * NX + x], x_dev(1)).wait_recv()

        @each(NX)
        def _(j):
            far(slot, slot, r2_ss.at[j, k], r_rs.at[k, c * NX + x], x_dev(j)).start()

        if k == 1:
            @each(NQ)
            def _(j):
                got = bcols.at[pl.ds(pl.multiple_of((q_of(NQ - j) * 2 + c) * 192, 64), 192), :]
                far(got, got, b_ss.at[j], b_rs.at[j], q_dev(j)).wait_recv()
                far(got, got, bf_ss.at[j], bf_rs.at[j], sib).start()

    gather(grad, gy, gfull, gy_ss, gy_rs, 0, during_first)

    @each(NQ, 0)
    def _(j):
        got = bcols.at[pl.ds(pl.multiple_of((q_of(NQ - j) * 2 + 1 - c) * 192, 64), 192), :]
        far(got, got, bf_ss.at[j], bf_rs.at[j], sib).wait_recv()

    rin = dot(gfull[...], bcols[...]).astype(BF)

    def e_block(ref, k, rows=slice(None)):
        return ref.at[rows, pl.ds(pl.multiple_of(q_of(k) * 384, 128), 384)]

    mine = pl.ds(pl.multiple_of(c * 48, 16), 48)
    other = pl.ds(pl.multiple_of((1 - c) * 48, 16), 48)

    @each(NQ, 0)
    def _(k):
        pt[...] = dot(rin, e_block(bg, k)[...], TN)
        keep[k] = pt[mine, :]
        half_s[k] = pt[other, :].astype(BF)
        far(half_s.at[k], half_r.at[k], h_ss.at[k], h_rs.at[k], sib).start()

    @each(NQ)
    def _(k):
        far(half_s.at[k], half_r.at[k], h_ss.at[k], h_rs.at[k], sib).wait_recv()
        rs_s[k] = (keep[k] + half_r[k].astype(F32)).astype(BF)
        far(rs_s.at[k], rs_r.at[k], p_ss.at[k], p_rs.at[k], q_dev(k)).start()

    far(half_s.at[0], half_r.at[0], h_ss.at[0], h_rs.at[0], sib).wait_recv()
    keep[0] = keep[0] + half_r[0].astype(F32)

    @each(NX, 0)
    def _(j):
        col = c * NX + lax.rem(x + NX - j, NX)

        @each(NY, 0)
        def _(k):
            slot = r_buf.at[k, col]

            @pl.when(j > 0)
            def _():
                far(slot, slot, r2_ss.at[j, k], r_rs.at[k, col], x_dev(j)).wait_recv()

            far(slot, slot, r3_ss.at[j, k], r_rs.at[k, col], sib).start()

    @each(NQ)
    def _(k):
        far(rs_s.at[k], rs_r.at[k], p_ss.at[k], p_rs.at[k], q_dev(k)).wait_recv()
        keep[0] = keep[0] + rs_r[k].astype(F32)

    denominator = sa[mine, :] * e_block(sg, 0)[...] + DAMPING
    sc_own = e_block(sc, 0, mine)
    sc_own[...] = (keep[0] / denominator).astype(BF)

    @each(NQ)
    def _(k):
        far(sc_own, sc_own, s_ss.at[k], s_rs.at[k], q_dev(k)).start()

    far(sc_own, sc_own, sf_ss.at[0], sf_rs.at[0], sib).start()

    @each(NX, 0)
    def _(j):
        col = (1 - c) * NX + j

        @each(NY, 0)
        def _(k):
            slot = r_buf.at[k, col]
            far(slot, slot, r3_ss.at[0, 0], r_rs.at[k, col], sib).wait_recv()

    @each(NY)
    def _(k):
        slot = c_buf.at[y_of(NY - k)]
        far(slot, slot, c_ss.at[k], c_rs.at[k], y_dev(k)).wait_recv()
        tile = cnt_y.at[y_of(NY - k)]
        far(tile, tile, n_ss.at[k], n_rs.at[k], y_dev(k)).wait_recv()

    cnt_s[...] = cnt_y[0] + cnt_y[1] + cnt_y[2] + cnt_y[3]

    @each(NZ, 0)
    def _(k):
        to = z_of(k)
        ta = jnp.zeros((96, 192), F32)
        tg = jnp.zeros((96, 192), F32)
        for i in range(NY):
            ta = ta + dot(r_buf[i, to, :, 0:256], c_buf[i, :, 0:256], NT)
            tg = tg + dot(r_buf[i, to, :, 256:512], c_buf[i, :, 256:512], NT)
        az_s[k] = jnp.concatenate([ta, tg], axis=1).astype(BF)
        bap[pl.ds(pl.multiple_of(to * 96, 32), 96), :] = lanes4(
            [r_buf[i, to, :, 512:608] for i in range(NY)]
        )

        @pl.when(k > 0)
        def _():
            far(az_s.at[k], az.at[k], a_ss.at[k], a_rs.at[k], z_dev(k)).start()
            far(cnt_s, cnt_z.at[k], m_ss.at[k], m_rs.at[k], z_dev(k)).start()

    @each(NQ)
    def _(k):
        got = e_block(sc, NQ - k, mine)
        far(got, got, s_ss.at[k], s_rs.at[k], q_dev(k)).wait_recv()
        far(got, got, sf_ss.at[k], sf_rs.at[k], sib).start()

    @each(NQ, 0)
    def _(k):
        got = e_block(sc, NQ - k, other)
        far(got, got, sf_ss.at[k], sf_rs.at[k], sib).wait_recv()

    boy_own = boy.at[y]
    boy_own[...] = dot(bg[...], sc[...], NT).astype(BF)

    @each(NY)
    def _(k):
        far(boy_own, boy_own, o_ss.at[k], o_rs.at[k], y_dev(k)).start()

    @each(NY)
    def _(k):
        slot = boy.at[y_of(NY - k)]
        far(slot, slot, o_ss.at[k], o_rs.at[k], y_dev(k)).wait_recv()

    back = lanes4([boy[i] for i in range(NY)])

    @each(NZ + 1)
    def _(k):
        to = z_of(k)
        part = dot(back, bap[pl.ds(pl.multiple_of(to * 96, 32), 96), :], NT)

        @pl.when(k < NZ)
        def _():
            pz_s[k] = part.astype(BF)
            far(pz_s.at[k], pz.at[k], z_ss.at[k], z_rs.at[k], z_dev(k)).start()

        @pl.when(k == NZ)
        def _():
            pz_s[0] = part.astype(BF)

    total = pz_s[0].astype(F32)
    pt_sum = total
    for k in range(1, NZ):
        far(pz_s.at[k], pz.at[k], z_ss.at[k], z_rs.at[k], z_dev(k)).wait_recv()
        pt_sum = pt_sum + pz[k].astype(F32)
    py_own = py.at[NY]
    py_own[...] = pt_sum.astype(BF)

    @each(NY)
    def _(k):
        far(py_own, py.at[y], q_ss.at[k], q_rs.at[k], y_dev(k)).start()

    def finish_factors(step):
        if step > 0:
            return

        @each(NZ)
        def _(k):
            far(az_s.at[k], az.at[k], a_ss.at[k], a_rs.at[k], z_dev(k)).wait_recv()
            far(cnt_s, cnt_z.at[k], m_ss.at[k], m_rs.at[k], z_dev(k)).wait_recv()

        stat = az_s[0].astype(F32)
        count = cnt_s[...]
        for k in range(1, NZ):
            stat = stat + az[k].astype(F32)
            count = count + cnt_z[k]
        scale = (1.0 - DECAY) / count[0:1, 0:1]
        fa_new[...] = DECAY * fa_old[...] + stat[:, 0:192] * scale
        fg_new[...] = DECAY * fg_old[...] + stat[:, 192:384] * scale

    gather(py_own, py, out, q_ss, q_rs, 1, finish_factors)

    @each(NY)
    def _(k):
        far(grad, gy.at[y], gy_ss.at[k], gy_rs.at[k], y_dev(k)).wait_send()
        far(c_own, c_own, c_ss.at[k], c_rs.at[k], y_dev(k)).wait_send()
        far(cnt_y.at[y], cnt_y.at[y], n_ss.at[k], n_rs.at[k], y_dev(k)).wait_send()
        far(boy_own, boy_own, o_ss.at[k], o_rs.at[k], y_dev(k)).wait_send()
        far(py_own, py.at[y], q_ss.at[k], q_rs.at[k], y_dev(k)).wait_send()

    @each(NQ)
    def _(k):
        far(ba, b_own, b_ss.at[k], b_rs.at[k], q_dev(k)).wait_send()
        far(rs_s.at[k], rs_r.at[k], p_ss.at[k], p_rs.at[k], q_dev(k)).wait_send()
        far(sc_own, sc_own, s_ss.at[k], s_rs.at[k], q_dev(k)).wait_send()
        far(az_s.at[k], az.at[k], a_ss.at[k], a_rs.at[k], z_dev(k)).wait_send()
        far(cnt_s, cnt_z.at[k], m_ss.at[k], m_rs.at[k], z_dev(k)).wait_send()
        far(pz_s.at[k], pz.at[k], z_ss.at[k], z_rs.at[k], z_dev(k)).wait_send()

    @each(NQ, 0)
    def _(k):
        far(ba, b_own, bf_ss.at[k], bf_rs.at[k], sib).wait_send()
        far(half_s.at[k], half_r.at[k], h_ss.at[k], h_rs.at[k], sib).wait_send()
        far(sc_own, sc_own, sf_ss.at[k], sf_rs.at[k], sib).wait_send()

    for h in range(2):
        for t in range(2):
            itself, src, dst, copy = piece(h, t)

            @pl.when(jnp.logical_not(itself))
            def _():
                copy.wait_send()

    @each(NY, 0)
    def _(k):
        slot = r_buf.at[k, q]

        @each(NX)
        def _(j):
            far(slot, slot, r2_ss.at[j, k], r_rs.at[k, q], x_dev(j)).wait_send()

        @each(NX, 0)
        def _(j):
            far(slot, slot, r3_ss.at[j, k], r_rs.at[k, q], sib).wait_send()

    for ring, full in ((0, gfull), (1, out)):
        for k in range(4):
            rows = 192 if k < 3 else 96
            for way in range(2):
                slot = full.at[pl.ds(0, rows), pl.ds(0, 384)]
                far(slot, slot, ring_ss.at[ring, way, k], ring_rs.at[ring, way, k], z_dev(1)).wait_send()


def local(
    layer_inputs,
    output_cotangents,
    valid,
    factor_a_old,
    factor_g_old,
    weight_gradient,
    basis_g,
    basis_a,
    spectrum_g,
    spectrum_a,
):
    V = pltpu.VMEM
    dma = pltpu.SemaphoreType.DMA
    scratch = [
        V((192, 640), BF),
        V((4, 8, 96, 640), BF),
        V((4, 192, 512), BF),
        V((768, 384), BF),
        V((8, 96, 384), BF),
        V((8, 96, 384), BF),
        V((4, 8, 128), F32),
        V((8, 128), F32),
        V((8, 8, 128), F32),
        V((4, 192, 96), BF),
        V((192, 3072), BF),
        V((3072, 96), BF),
        V((96, 384), F32),
        V((8, 48, 384), BF),
        V((8, 48, 384), BF),
        V((8, 48, 384), F32),
        V((8, 48, 384), BF),
        V((8, 48, 384), BF),
        V((96, 3072), BF),
        V((4, 192, 96), BF),
        V((8, 192, 96), BF),
        V((8, 192, 96), BF),
        V((5, 192, 96), BF),
        dma((4,)), dma((4,)),
        dma((2, 2, 4)), dma((2, 2, 4)),
        dma((8,)), dma((8,)), dma((8,)), dma((8,)),
        dma((4,)), dma((4, 4)), dma((4, 4)), dma((4, 8)),
        dma((4,)), dma((4,)), dma((4,)), dma((4,)), dma((8,)), dma((8,)),
        dma((8,)), dma((8,)), dma((8,)), dma((8,)), dma((8,)), dma((8,)), dma((8,)), dma((8,)),
        dma((8,)), dma((8,)), dma((4,)), dma((4,)), dma((8,)), dma((8,)), dma((4,)), dma((4,)),
    ]
    return pl.pallas_call(
        kernel,
        out_shape=(
            jax.ShapeDtypeStruct((96, 192), F32),
            jax.ShapeDtypeStruct((96, 192), F32),
            jax.ShapeDtypeStruct((192, 3072), BF),
        ),
        in_specs=[pl.BlockSpec(memory_space=V)] * 10,
        out_specs=(pl.BlockSpec(memory_space=V),) * 3,
        scratch_shapes=scratch,
        compiler_params=pltpu.CompilerParams(
            collective_id=0, has_side_effects=True, vmem_limit_bytes=48 * 1024 * 1024
        ),
    )(
        layer_inputs.T,
        output_cotangents.T,
        valid[None, :],
        factor_a_old,
        factor_g_old,
        weight_gradient,
        basis_g,
        basis_a,
        spectrum_g[None, :],
        spectrum_a[:, None],
    )


def solution(mesh):
    placed = (
        P("rep", "shard"),
        P("rep", "shard"),
        P("rep"),
        P("rep", "shard"),
        P("rep", "shard"),
        P("shard", "rep"),
        P("shard", None),
        P("shard", "rep"),
        P(),
        P("rep"),
    )
    return jax.shard_map(
        local,
        mesh=mesh,
        in_specs=placed,
        out_specs=(P("rep", "shard"), P("rep", "shard"), P("shard", None)),
        check_vma=False,
    )
```

```python
import jax
import jax.numpy as jnp
from jax import lax
from jax.experimental import pallas as pl
from jax.experimental.pallas import tpu as pltpu
from jax.sharding import PartitionSpec as P

DAMPING = 0.03
DECAY = 0.95

NZ, NY, NQ, NX = 8, 4, 8, 4
BF, F32 = jnp.bfloat16, jnp.float32
NT = (((1,), (1,)), ((), ()))


def dot(a, b, dims=(((1,), (0,)), ((), ()))):
    return lax.dot_general(a, b, dims, preferred_element_type=F32)


def lanes4(parts):
    return jnp.concatenate([p.astype(F32) for p in parts], axis=1).astype(BF)


def kernel(
    xa_in, xg_in, valid_in, fa_in, fg_in, grad_in, bg_in, ba_in, sg_in, sa_in,
    fa_out, fg_out, out_hbm,
    fa_new, fg_new, out, out_sems,
    xa, xg, valid, fa_old, fg_old, grad, bg, ba, sg, sa, in_sems, sa_col,
    d_buf, r_buf, c_buf, b_buf, r_ba, az_s, az, cnt_y, cnt_s, cnt_z,
    gz, rp_s, rp_r, pt, half_s, half_r, keep, rs_s, rs_r, sc,
    back, boy, pz_s, pz, py,
    gy_ss, gy_rs, g_ss, g_rs, f_ss, f_rs, rb1_ss, rb2_ss, rb3_ss, rb_rs,
    r1_ss, r2_ss, r3_ss, r_rs, c_ss, c_rs, n_ss, n_rs, m_ss, m_rs,
    h_ss, h_rs, p_ss, p_rs, s_ss, s_rs, sf_ss, sf_rs,
    a_ss, a_rs, o_ss, o_rs, z_ss, z_rs, q_ss, q_rs,
):
    r = lax.axis_index("rep")
    s = lax.axis_index("shard")
    z, y = lax.div(r, NY), lax.rem(r, NY)
    q, c = lax.div(s, 2), lax.rem(s, 2)
    yh, x = lax.div(q, NX), lax.rem(q, NX)
    half = lax.div(y, 2)

    def y_of(k):
        return lax.rem(y + k, NY)

    def z_of(k):
        return lax.rem(z + k, NZ)

    def q_of(k):
        return lax.rem(q + k, NQ)

    def y_dev(k):
        return (z * NY + y_of(k), s)

    def z_dev(k):
        return (z_of(k) * NY + y, s)

    def q_dev(k):
        return (r, q_of(k) * 2 + c)

    def x_dev(k):
        return (r, (yh * NX + lax.rem(x + k, NX)) * 2 + c)

    sib = (r, q * 2 + 1 - c)

    def far(src, dst, ss, rs, dev):
        return pltpu.make_async_remote_copy(
            src_ref=src, dst_ref=dst, send_sem=ss, recv_sem=rs,
            device_id=dev, device_id_type=pl.DeviceIdType.MESH,
        )

    def each(n, first=1):
        def deco(body):
            def step(k, carry):
                body(k)
                return carry
            lax.fori_loop(first, n, step, 0)
        return deco

    loads = [
        pltpu.make_async_copy(src, dst, in_sems.at[i])
        for i, (src, dst) in enumerate((
            (grad_in, grad), (ba_in, ba), (xa_in, xa), (xg_in, xg), (valid_in, valid),
            (bg_in, bg), (sg_in, sg), (sa_in, sa), (fa_in, fa_old), (fg_in, fg_old),
        ))
    ]
    for load in loads:
        load.start()

    gate = pltpu.get_barrier_semaphore()

    def greet(dev):
        pl.semaphore_signal(gate, inc=1, device_id=dev, device_id_type=pl.DeviceIdType.MESH)

    each(NY)(lambda k: greet(y_dev(k)))
    each(NZ)(lambda k: greet(z_dev(k)))
    each(NQ)(lambda k: greet(q_dev(k)))
    greet(sib)
    own_piece = jnp.logical_and(half == c, yh == c)

    @each(NY, 0)
    def _(j):
        itself = jnp.logical_and(own_piece, j == y)

        @pl.when(jnp.logical_not(itself))
        def _():
            greet((z * NY + j, (c * NX + x) * 2 + half))

    c_own = c_buf.at[y]
    b_own = b_buf
    for load in loads[:5]:
        load.wait()
    g_own = gz.at[:, pl.ds(pl.multiple_of(z * 128, 128), 128)]
    g_own[:, 0:96] = grad[...]
    g_own[:, 96:128] = jnp.zeros((192, 32), BF)
    b_own[:, 0:96] = ba[...]
    b_own[:, 96:128] = jnp.zeros((192, 32), BF)
    for i in range(NQ):
        r_ba[128 * i + 96 : 128 * i + 128, :] = jnp.zeros((32, 512), BF)
    m = valid[...].reshape(1, 256).astype(F32)
    d_buf[:, 0:256] = xa[...]
    d_buf[:, 256:512] = xg[...]

    pl.semaphore_wait(gate, 3 + 7 + 7 + 1 + 4 - jnp.where(own_piece, 1, 0))

    class Plane:
        def __init__(self, src, slot, ss1, ss2, ss3, rs):
            self.src, self.slot, self.ss1, self.ss2, self.ss3, self.rs = src, slot, ss1, ss2, ss3, rs

        def piece(self, h, t):
            dev = (z * NY + 2 * c + h, (t * NX + x) * 2 + yh)
            itself = jnp.logical_and(dev[0] == r, dev[1] == s)
            src, dst = self.src.at[pl.ds(96 * h, 96), :], self.slot(y, q)
            return itself, src, dst, far(src, dst, self.ss1.at[2 * h + t], self.rs.at[y, q], dev)

        def along_y(self):
            for h in range(2):
                for t in range(2):
                    itself, src, dst, copy = self.piece(h, t)

                    @pl.when(jnp.logical_not(itself))
                    def _():
                        copy.start()

                    @pl.when(itself)
                    def _():
                        pltpu.make_async_copy(src, dst, self.rs.at[y, q]).start()

        def along_x(self, k):
            slot = self.slot(k, c * NX + x)
            far(slot, slot, self.ss2.at[0, k], self.rs.at[k, c * NX + x], x_dev(1)).wait_recv()

            @each(NX)
            def _(j):
                far(slot, slot, self.ss2.at[j, k], self.rs.at[k, c * NX + x], x_dev(j)).start()

            far(slot, slot, self.ss3.at[0, k], self.rs.at[k, c * NX + x], sib).start()

        def to_core(self):
            @each(NX)
            def _(j):
                col = c * NX + lax.rem(x + NX - j, NX)

                @each(NY, 0)
                def _(k):
                    slot = self.slot(k, col)
                    far(slot, slot, self.ss2.at[j, k], self.rs.at[k, col], x_dev(j)).wait_recv()
                    far(slot, slot, self.ss3.at[j, k], self.rs.at[k, col], sib).start()

        def arrive(self):
            @each(NX, 0)
            def _(j):
                col = (1 - c) * NX + j

                @each(NY, 0)
                def _(k):
                    slot = self.slot(k, col)
                    far(slot, slot, self.ss3.at[0, 0], self.rs.at[k, col], sib).wait_recv()

        def sent(self):
            for h in range(2):
                for t in range(2):
                    itself, src, dst, copy = self.piece(h, t)

                    @pl.when(jnp.logical_not(itself))
                    def _():
                        copy.wait_send()

            @each(NY, 0)
            def _(k):
                slot = self.slot(k, q)

                @each(NX)
                def _(j):
                    far(slot, slot, self.ss2.at[j, k], self.rs.at[k, q], x_dev(j)).wait_send()

                @each(NX, 0)
                def _(j):
                    far(slot, slot, self.ss3.at[j, k], self.rs.at[k, q], sib).wait_send()

    def ba_slot(k, col):
        return r_ba.at[pl.ds(pl.multiple_of(col * 128, 128), 96), pl.ds(pl.multiple_of(k * 128, 128), 128)]

    rows_b = Plane(b_own, ba_slot, rb1_ss, rb2_ss, rb3_ss, rb_rs)
    rows_x = Plane(d_buf, lambda k, col: r_buf.at[k, col], r1_ss, r2_ss, r3_ss, r_rs)

    def during_first(k):
        if k == 0:
            rows_b.along_y()
            c_own[:, 0:256] = (xa[...].astype(F32) * m).astype(BF)
            c_own[:, 256:512] = (xg[...].astype(F32) * m).astype(BF)
            cnt_y[y] = jnp.broadcast_to(jnp.sum(m, axis=1, keepdims=True), (8, 128))
        else:
            rows_b.along_x(k - 1)

    @each(NZ)
    def _(k):
        far(g_own, g_own, g_ss.at[k], g_rs.at[k], z_dev(k)).start()

    for k in range(4):
        during_first(k)
    rows_b.along_x(3)
    rows_x.along_y()
    rows_b.to_core()
    rows_b.arrive()

    @each(NZ)
    def _(k):
        got = gz.at[:, pl.ds(pl.multiple_of(z_of(NZ - k) * 128, 128), 128)]
        far(got, got, g_ss.at[k], g_rs.at[k], z_dev(k)).wait_recv()

    def cols_copies(d):
        for way, sign, ok, end in ((0, -1, y >= d, y < NY - 1), (1, 1, y + d < NY, y > 0)):
            slot = c_buf.at[jnp.clip(y + sign * d, 0, NY - 1)]
            who = jnp.clip(y + sign * d, 0, NY - 1)
            to = (jnp.clip(y - sign, 0, NY - 1) + z * NY, s)
            yield ok, jnp.logical_and(ok, end), far(slot, slot, c_ss.at[way, d], c_rs.at[who], to)

    def cols_step(d):
        for ok, onward, copy in cols_copies(d):
            if d > 0:
                pl.when(ok)(copy.wait_recv)
            if d < NY - 1:
                pl.when(onward)(copy.start)

    def y_lanes(ref, i):
        return ref.at[:, pl.ds(pl.multiple_of(i * 128, 128), 128)]

    @each(NY + 1)
    def _(k):
        to = y_of(k)
        y_lanes(rp_s, to)[...] = dot(gz[...], y_lanes(r_ba, to)[...]).astype(BF)

        @pl.when(k < NY)
        def _():
            far(y_lanes(rp_s, to), rp_r.at[k], gy_ss.at[k], gy_rs.at[k], y_dev(k)).start()

    rin = y_lanes(rp_s, y)[...].astype(F32)
    for k in range(1, NY):
        far(y_lanes(rp_s, y), rp_r.at[k], gy_ss.at[k], gy_rs.at[k], y_dev(k)).wait_recv()
        rin = rin + rp_r[k].astype(F32)
    rin = rin.T[0:96, :].astype(BF)

    for load in loads[5:]:
        load.wait()
    sa_row = jnp.concatenate([sa[...].reshape(1, 96), jnp.zeros((1, 32), F32)], axis=1)
    sa_col[...] = jnp.broadcast_to(sa_row, (128, 128)).T[0:96, 0:1]

    def e_block(ref, k, rows=slice(None)):
        return ref.at[rows, pl.ds(pl.multiple_of(q_of(k) * 384, 128), 384)]

    mine = pl.ds(pl.multiple_of(c * 48, 16), 48)
    other = pl.ds(pl.multiple_of((1 - c) * 48, 16), 48)

    @each(NQ, 0)
    def _(k):
        pt[...] = dot(rin, e_block(bg, k)[...])
        keep[k] = pt[mine, :]
        half_s[k] = pt[other, :].astype(BF)
        far(half_s.at[k], half_r.at[k], h_ss.at[k], h_rs.at[k], sib).start()

    @each(NQ)
    def _(k):
        far(half_s.at[k], half_r.at[k], h_ss.at[k], h_rs.at[k], sib).wait_recv()
        rs_s[k] = (keep[k] + half_r[k].astype(F32)).astype(BF)
        far(rs_s.at[k], rs_r.at[k], p_ss.at[k], p_rs.at[k], q_dev(k)).start()

    cols_step(0)

    @each(NY)
    def _(k):
        far(cnt_y.at[y], cnt_y.at[y], n_ss.at[k], n_rs.at[k], y_dev(k)).start()

    far(half_s.at[0], half_r.at[0], h_ss.at[0], h_rs.at[0], sib).wait_recv()
    keep[0] = keep[0] + half_r[0].astype(F32)

    @each(NY, 0)
    def _(k):
        rows_x.along_x(k)

    @each(NQ)
    def _(k):
        far(rs_s.at[k], rs_r.at[k], p_ss.at[k], p_rs.at[k], q_dev(k)).wait_recv()
        keep[0] = keep[0] + rs_r[k].astype(F32)

    sg_here = sg[pl.ds(pl.multiple_of(q * 384, 128), 384)].reshape(1, 384)
    denominator = sa_col[mine, :] * sg_here + DAMPING
    sc_own = e_block(sc, 0, mine)
    sc_own[...] = (keep[0] / denominator).astype(BF)

    @each(NQ)
    def _(k):
        far(sc_own, sc_own, s_ss.at[k], s_rs.at[k], q_dev(k)).start()

    far(sc_own, sc_own, sf_ss.at[0], sf_rs.at[0], sib).start()

    cols_step(1)

    @each(NQ)
    def _(k):
        got = e_block(sc, NQ - k, mine)
        far(got, got, s_ss.at[k], s_rs.at[k], q_dev(k)).wait_recv()
        far(got, got, sf_ss.at[k], sf_rs.at[k], sib).start()

    back[...] = jnp.zeros((192, 96), F32)

    @each(NQ, 0)
    def _(k):
        got = e_block(sc, NQ - k, other)
        far(got, got, sf_ss.at[k], sf_rs.at[k], sib).wait_recv()
        back[...] += dot(e_block(bg, NQ - k)[...], e_block(sc, NQ - k)[...], NT)

    boy_own = y_lanes(boy, y)
    boy_own[:, 0:96] = back[...].astype(BF)
    boy_own[:, 96:128] = jnp.zeros((192, 32), BF)

    @each(NY)
    def _(k):
        far(boy_own, boy_own, o_ss.at[k], o_rs.at[k], y_dev(k)).start()

    cols_step(2)

    @each(NY)
    def _(k):
        slot = y_lanes(boy, y_of(NY - k))
        far(slot, slot, o_ss.at[k], o_rs.at[k], y_dev(k)).wait_recv()

    def pz_half(h, k):
        rows = pl.ds(96 * h, 96)
        return far(pz_s.at[k, rows, :], pz.at[k, rows, :], z_ss.at[h, k], z_rs.at[h, k], z_dev(k))

    @each(NZ + 1)
    def _(k):
        to = z_of(k)
        rows = r_ba[pl.ds(pl.multiple_of(to * 128, 128), 128), :]
        pz_s[k] = dot(boy[...], rows, NT).astype(BF)

        @pl.when(k < NZ)
        def _():
            pz_half(0, k).start()

    each(NZ)(lambda k: pz_half(1, k).start())

    rows_x.to_core()
    rows_x.arrive()

    @each(NY)
    def _(k):
        tile = cnt_y.at[y_of(NY - k)]
        far(tile, tile, n_ss.at[k], n_rs.at[k], y_dev(k)).wait_recv()

    cols_step(3)
    cnt_s[...] = cnt_y[0] + cnt_y[1] + cnt_y[2] + cnt_y[3]

    @each(NZ, 0)
    def _(k):
        to = z_of(k)
        ta = jnp.zeros((96, 192), F32)
        tg = jnp.zeros((96, 192), F32)
        for i in range(NY):
            ta = ta + dot(r_buf[i, to, :, 0:256], c_buf[i, :, 0:256], NT)
            tg = tg + dot(r_buf[i, to, :, 256:512], c_buf[i, :, 256:512], NT)
        az_s[k] = jnp.concatenate([ta, tg], axis=1).astype(BF)

        @pl.when(k > 0)
        def _():
            far(az_s.at[k], az.at[k], a_ss.at[k], a_rs.at[k], z_dev(k)).start()
            far(cnt_s, cnt_z.at[k], m_ss.at[k], m_rs.at[k], z_dev(k)).start()

    def py_half(h, k):
        slot = py.at[y, pl.ds(96 * h, 96), :]
        return far(slot, slot, q_ss.at[h, k], q_rs.at[h, k], y_dev(k))

    for h in range(2):
        rows = slice(96 * h, 96 * h + 96)
        total = pz_s[NZ, rows, :].astype(F32)
        for k in range(1, NZ):
            pz_half(h, k).wait_recv()
            total = total + pz[k, rows, :].astype(F32)
        py[y, rows, :] = total.astype(BF)
        each(NY)(lambda k: py_half(h, k).start())

    def store(i):
        block = pl.ds(pl.multiple_of(z_of(i) * 384, 128), 384)
        return pltpu.make_async_copy(out.at[:, block], out_hbm.at[:, block], out_sems.at[i])

    fa_store = pltpu.make_async_copy(fa_new, fa_out, out_sems.at[8])
    fg_store = pltpu.make_async_copy(fg_new, fg_out, out_sems.at[9])

    def finish_factors(step):
        if step > 0:
            store(step).start()
            store(NZ - step).start()
            return
        store(0).start()

        @each(NZ)
        def _(k):
            far(az_s.at[k], az.at[k], a_ss.at[k], a_rs.at[k], z_dev(k)).wait_recv()
            far(cnt_s, cnt_z.at[k], m_ss.at[k], m_rs.at[k], z_dev(k)).wait_recv()

        stat = az_s[0].astype(F32)
        count = cnt_s[...]
        for k in range(1, NZ):
            stat = stat + az[k].astype(F32)
            count = count + cnt_z[k]
        scale = (1.0 - DECAY) / count[0:1, 0:1]
        fa_new[...] = DECAY * fa_old[...] + stat[:, 0:192] * scale
        fg_new[...] = DECAY * fg_old[...] + stat[:, 192:384] * scale
        fa_store.start()
        fg_store.start()

    def ring_copy(h, way, k, arriving):
        at = z_of((NZ - 1, 1)[way] * (k + arriving))
        lo, n = (96 * h, 96) if k < 3 else (96 * h + 48 * way, 48)
        slot = out.at[pl.ds(lo, n), pl.ds(pl.multiple_of(at * 384, 128), 384)]
        return far(slot, slot, f_ss.at[h, way, k], f_rs.at[h, way, k], z_dev((1, NZ - 1)[way]))

    for k in range(5):
        for h in range(2):
            if k == 0:
                rows = pl.ds(96 * h, 96)
                for j in range(1, NY):
                    py_half(h, j).wait_recv()
                out[rows, pl.ds(pl.multiple_of(z * 384, 128), 384)] = lanes4(
                    [py[i, 96 * h : 96 * h + 96, 0:96] for i in range(NY)]
                )
            for way in range(2):
                if k > 0:
                    ring_copy(h, way, k - 1, 1).wait_recv()
                if k < 4:
                    ring_copy(h, way, k, 0).start()
        if k < 4:
            finish_factors(k)
    store(4).start()

    for i in range(NZ):
        store(i).wait()
    fa_store.wait()
    fg_store.wait()

    @each(NY)
    def _(k):
        far(y_lanes(rp_s, y), rp_r.at[k], gy_ss.at[k], gy_rs.at[k], y_dev(k)).wait_send()
        far(cnt_y.at[y], cnt_y.at[y], n_ss.at[k], n_rs.at[k], y_dev(k)).wait_send()
        far(boy_own, boy_own, o_ss.at[k], o_rs.at[k], y_dev(k)).wait_send()
        py_half(0, k).wait_send()
        py_half(1, k).wait_send()

    @each(NQ)
    def _(k):
        far(rs_s.at[k], rs_r.at[k], p_ss.at[k], p_rs.at[k], q_dev(k)).wait_send()
        far(sc_own, sc_own, s_ss.at[k], s_rs.at[k], q_dev(k)).wait_send()
        far(g_own, g_own, g_ss.at[k], g_rs.at[k], z_dev(k)).wait_send()
        far(az_s.at[k], az.at[k], a_ss.at[k], a_rs.at[k], z_dev(k)).wait_send()
        far(cnt_s, cnt_z.at[k], m_ss.at[k], m_rs.at[k], z_dev(k)).wait_send()
        pz_half(0, k).wait_send()
        pz_half(1, k).wait_send()

    @each(NQ, 0)
    def _(k):
        far(half_s.at[k], half_r.at[k], h_ss.at[k], h_rs.at[k], sib).wait_send()
        far(sc_own, sc_own, sf_ss.at[k], sf_rs.at[k], sib).wait_send()

    for d in range(NY - 1):
        for ok, onward, copy in cols_copies(d):
            pl.when(onward)(copy.wait_send)

    rows_b.sent()
    rows_x.sent()

    for h in range(2):
        for way in range(2):
            for k in range(4):
                ring_copy(h, way, k, 0).wait_send()


def local(
    layer_inputs,
    output_cotangents,
    valid,
    factor_a_old,
    factor_g_old,
    weight_gradient,
    basis_g,
    basis_a,
    spectrum_g,
    spectrum_a,
):
    V = pltpu.VMEM
    dma = pltpu.SemaphoreType.DMA
    scratch = [
        V((96, 192), F32), V((96, 192), F32), V((192, 3072), BF), dma((10,)),
        V((192, 256), BF), V((192, 256), BF), V((256,), jnp.int32),
        V((96, 192), F32), V((96, 192), F32), V((192, 96), BF),
        V((192, 3072), BF), V((192, 96), BF), V((3072,), F32), V((96,), F32), dma((10,)),
        V((96, 1), F32),
        V((192, 512), BF),
        V((4, 8, 96, 512), BF),
        V((4, 192, 512), BF),
        V((192, 128), BF),
        V((1024, 512), BF),
        V((8, 96, 384), BF),
        V((8, 96, 384), BF),
        V((4, 8, 128), F32),
        V((8, 128), F32),
        V((8, 8, 128), F32),
        V((192, 1024), BF),
        V((192, 512), BF),
        V((4, 192, 128), BF),
        V((96, 384), F32),
        V((8, 48, 384), BF),
        V((8, 48, 384), BF),
        V((8, 48, 384), F32),
        V((8, 48, 384), BF),
        V((8, 48, 384), BF),
        V((96, 3072), BF),
        V((192, 96), F32),
        V((192, 512), BF),
        V((9, 192, 128), BF),
        V((8, 192, 128), BF),
        V((4, 192, 128), BF),
        dma((4,)), dma((4,)),
        dma((8,)), dma((8,)), dma((2, 2, 4)), dma((2, 2, 4)),
        dma((4,)), dma((4, 4)), dma((4, 4)), dma((4, 8)),
        dma((4,)), dma((4, 4)), dma((4, 4)), dma((4, 8)),
        dma((2, 4)), dma((4,)), dma((4,)), dma((4,)), dma((8,)), dma((8,)),
        dma((8,)), dma((8,)), dma((8,)), dma((8,)), dma((8,)), dma((8,)), dma((8,)), dma((8,)),
        dma((8,)), dma((8,)), dma((4,)), dma((4,)), dma((2, 8)), dma((2, 8)), dma((2, 4)), dma((2, 4)),
    ]
    return pl.pallas_call(
        kernel,
        out_shape=(
            jax.ShapeDtypeStruct((96, 192), F32),
            jax.ShapeDtypeStruct((96, 192), F32),
            jax.ShapeDtypeStruct((192, 3072), BF),
        ),
        in_specs=[pl.BlockSpec(memory_space=pltpu.HBM)] * 10,
        out_specs=(pl.BlockSpec(memory_space=pltpu.HBM),) * 3,
        scratch_shapes=scratch,
        compiler_params=pltpu.CompilerParams(
            collective_id=0, has_side_effects=True, vmem_limit_bytes=62 * 1024 * 1024
        ),
    )(
        layer_inputs.T,
        output_cotangents.T,
        valid,
        factor_a_old,
        factor_g_old,
        weight_gradient,
        basis_g,
        basis_a,
        spectrum_g,
        spectrum_a,
    )


def solution(mesh):
    placed = (
        P("rep", "shard"),
        P("rep", "shard"),
        P("rep"),
        P("rep", "shard"),
        P("rep", "shard"),
        P("shard", "rep"),
        P("shard", None),
        P("shard", "rep"),
        P(),
        P("rep"),
    )
    return jax.shard_map(
        local,
        mesh=mesh,
        in_specs=placed,
        out_specs=(P("rep", "shard"), P("rep", "shard"), P("shard", None)),
        check_vma=False,
    )
```

```python
import jax
import jax.numpy as jnp
from jax import lax
from jax.experimental import pallas as pl
from jax.experimental.pallas import tpu as pltpu
from jax.sharding import PartitionSpec as P

DAMPING = 0.03
DECAY = 0.95

NZ, NY, NQ, NX = 8, 4, 8, 4
BF, F32 = jnp.bfloat16, jnp.float32
NT = (((1,), (1,)), ((), ()))


def dot(a, b, dims=(((1,), (0,)), ((), ()))):
    return lax.dot_general(a, b, dims, preferred_element_type=F32)


def lanes4(parts):
    return jnp.concatenate([p.astype(F32) for p in parts], axis=1).astype(BF)


def kernel(
    xa_in, xg_in, valid_in, fa_in, fg_in, grad_in, bg_in, ba_in, sg_in, sa_in,
    fa_new, fg_new, out,
    xa, xg, valid, fa_old, fg_old, grad, bg, ba, sg, sa, in_sems, sa_col,
    d_buf, r_buf, c_buf, b_buf, r_ba, acc, az_s, az, cnt_y, cnt_s, cnt_z,
    gz, rp_s, rp_r, pt, half_s, half_r, keep, rs_s, rs_r, sc,
    back, boy, pz_s, pz, py,
    gy_ss, gy_rs, g_ss, g_rs, f_ss, f_rs, rb1_ss, rb2_ss, rb3_ss, rb_rs,
    r1_ss, r2_ss, r3_ss, r_rs, c_ss, c_rs, n_ss, n_rs, m_ss, m_rs,
    h_ss, h_rs, p_ss, p_rs, s_ss, s_rs, sf_ss, sf_rs,
    a_ss, a_rs, o_ss, o_rs, z_ss, z_rs, q_ss, q_rs,
):
    r = lax.axis_index("rep")
    s = lax.axis_index("shard")
    z, y = lax.div(r, NY), lax.rem(r, NY)
    q, c = lax.div(s, 2), lax.rem(s, 2)
    yh, x = lax.div(q, NX), lax.rem(q, NX)
    half = lax.div(y, 2)

    def y_of(k):
        return lax.rem(y + k, NY)

    def z_of(k):
        return lax.rem(z + k, NZ)

    def q_of(k):
        return lax.rem(q + k, NQ)

    def y_dev(k):
        return (z * NY + y_of(k), s)

    def z_dev(k):
        return (z_of(k) * NY + y, s)

    def q_dev(k):
        return (r, q_of(k) * 2 + c)

    def x_dev(k):
        return (r, (yh * NX + lax.rem(x + k, NX)) * 2 + c)

    sib = (r, q * 2 + 1 - c)

    def far(src, dst, ss, rs, dev):
        return pltpu.make_async_remote_copy(
            src_ref=src, dst_ref=dst, send_sem=ss, recv_sem=rs,
            device_id=dev, device_id_type=pl.DeviceIdType.MESH,
        )

    def each(n, first=1):
        def deco(body):
            def step(k, carry):
                body(k)
                return carry
            lax.fori_loop(first, n, step, 0)
        return deco

    loads = [
        pltpu.make_async_copy(src, dst, in_sems.at[i])
        for i, (src, dst) in enumerate((
            (grad_in, grad), (ba_in, ba), (xa_in, xa), (xg_in, xg), (valid_in, valid),
            (bg_in, bg), (sg_in, sg), (sa_in, sa), (fa_in, fa_old), (fg_in, fg_old),
        ))
    ]
    for load in loads:
        load.start()

    gate = pltpu.get_barrier_semaphore()

    def greet(dev):
        pl.semaphore_signal(gate, inc=1, device_id=dev, device_id_type=pl.DeviceIdType.MESH)

    each(NY)(lambda k: greet(y_dev(k)))
    each(NZ)(lambda k: greet(z_dev(k)))
    each(NQ)(lambda k: greet(q_dev(k)))
    greet(sib)
    own_piece = jnp.logical_and(half == c, yh == c)

    @each(NY, 0)
    def _(j):
        itself = jnp.logical_and(own_piece, j == y)

        @pl.when(jnp.logical_not(itself))
        def _():
            greet((z * NY + j, (c * NX + x) * 2 + half))

    c_own = c_buf.at[y]
    b_own = b_buf
    for load in loads[:5]:
        load.wait()
    g_own = gz.at[:, pl.ds(pl.multiple_of(z * 128, 128), 128)]
    g_own[:, 0:96] = grad[...]
    g_own[:, 96:128] = jnp.zeros((192, 32), BF)
    b_own[:, 0:96] = ba[...]
    b_own[:, 96:128] = jnp.zeros((192, 32), BF)
    for i in range(NQ):
        r_ba[128 * i + 96 : 128 * i + 128, :] = jnp.zeros((32, 512), BF)
    m = valid[...].reshape(1, 256).astype(F32)
    d_buf[:, 0:256] = xa[...]
    d_buf[:, 256:512] = xg[...]

    pl.semaphore_wait(gate, 3 + 7 + 7 + 1 + 4 - jnp.where(own_piece, 1, 0))

    class Plane:
        def __init__(self, src, slot, ss1, ss2, ss3, rs):
            self.src, self.slot, self.ss1, self.ss2, self.ss3, self.rs = src, slot, ss1, ss2, ss3, rs

        def piece(self, h, t):
            dev = (z * NY + 2 * c + h, (t * NX + x) * 2 + yh)
            itself = jnp.logical_and(dev[0] == r, dev[1] == s)
            src, dst = self.src.at[pl.ds(96 * h, 96), :], self.slot(y, q)
            return itself, src, dst, far(src, dst, self.ss1.at[2 * h + t], self.rs.at[y, q], dev)

        def along_y(self):
            for h in range(2):
                for t in range(2):
                    itself, src, dst, copy = self.piece(h, t)

                    @pl.when(jnp.logical_not(itself))
                    def _():
                        copy.start()

                    @pl.when(itself)
                    def _():
                        pltpu.make_async_copy(src, dst, self.rs.at[y, q]).start()

        def along_x(self, k):
            slot = self.slot(k, c * NX + x)
            far(slot, slot, self.ss2.at[0, k], self.rs.at[k, c * NX + x], x_dev(1)).wait_recv()

            @each(NX)
            def _(j):
                far(slot, slot, self.ss2.at[j, k], self.rs.at[k, c * NX + x], x_dev(j)).start()

            far(slot, slot, self.ss3.at[0, k], self.rs.at[k, c * NX + x], sib).start()

        def to_core(self):
            @each(NX)
            def _(j):
                col = c * NX + lax.rem(x + NX - j, NX)

                @each(NY, 0)
                def _(k):
                    slot = self.slot(k, col)
                    far(slot, slot, self.ss2.at[j, k], self.rs.at[k, col], x_dev(j)).wait_recv()
                    far(slot, slot, self.ss3.at[j, k], self.rs.at[k, col], sib).start()

        def arrive(self):
            @each(NX, 0)
            def _(j):
                col = (1 - c) * NX + j

                @each(NY, 0)
                def _(k):
                    slot = self.slot(k, col)
                    far(slot, slot, self.ss3.at[0, 0], self.rs.at[k, col], sib).wait_recv()

        def sent(self):
            for h in range(2):
                for t in range(2):
                    itself, src, dst, copy = self.piece(h, t)

                    @pl.when(jnp.logical_not(itself))
                    def _():
                        copy.wait_send()

            @each(NY, 0)
            def _(k):
                slot = self.slot(k, q)

                @each(NX)
                def _(j):
                    far(slot, slot, self.ss2.at[j, k], self.rs.at[k, q], x_dev(j)).wait_send()

                @each(NX, 0)
                def _(j):
                    far(slot, slot, self.ss3.at[j, k], self.rs.at[k, q], sib).wait_send()

    def ba_slot(k, col):
        return r_ba.at[pl.ds(pl.multiple_of(col * 128, 128), 96), pl.ds(pl.multiple_of(k * 128, 128), 128)]

    rows_b = Plane(b_own, ba_slot, rb1_ss, rb2_ss, rb3_ss, rb_rs)
    rows_x = Plane(d_buf, lambda k, col: r_buf.at[k, col], r1_ss, r2_ss, r3_ss, r_rs)

    def during_first(k):
        if k == 0:
            rows_b.along_y()
            c_own[:, 0:256] = (xa[...].astype(F32) * m).astype(BF)
            c_own[:, 256:512] = (xg[...].astype(F32) * m).astype(BF)
            cnt_y[y] = jnp.broadcast_to(jnp.sum(m, axis=1, keepdims=True), (8, 128))
        else:
            rows_b.along_x(k - 1)

    @each(NZ)
    def _(k):
        far(g_own, g_own, g_ss.at[k], g_rs.at[k], z_dev(k)).start()

    for k in range(4):
        during_first(k)
    rows_b.along_x(3)
    rows_x.along_y()
    rows_b.to_core()
    rows_b.arrive()

    @each(NZ)
    def _(k):
        got = gz.at[:, pl.ds(pl.multiple_of(z_of(NZ - k) * 128, 128), 128)]
        far(got, got, g_ss.at[k], g_rs.at[k], z_dev(k)).wait_recv()

    def cols_copies(d):
        for way, sign, ok, end in ((0, -1, y >= d, y < NY - 1), (1, 1, y + d < NY, y > 0)):
            slot = c_buf.at[jnp.clip(y + sign * d, 0, NY - 1)]
            who = jnp.clip(y + sign * d, 0, NY - 1)
            to = (jnp.clip(y - sign, 0, NY - 1) + z * NY, s)
            yield ok, jnp.logical_and(ok, end), far(slot, slot, c_ss.at[way, d], c_rs.at[who], to)

    def cols_step(d):
        for ok, onward, copy in cols_copies(d):
            if d > 0:
                pl.when(ok)(copy.wait_recv)
            if d < NY - 1:
                pl.when(onward)(copy.start)

    def y_lanes(ref, i):
        return ref.at[:, pl.ds(pl.multiple_of(i * 128, 128), 128)]

    @each(NY + 1)
    def _(k):
        to = y_of(k)
        y_lanes(rp_s, to)[...] = dot(gz[...], y_lanes(r_ba, to)[...]).astype(BF)

        @pl.when(k < NY)
        def _():
            far(y_lanes(rp_s, to), rp_r.at[k], gy_ss.at[k], gy_rs.at[k], y_dev(k)).start()

    @each(NY, 0)
    def _(k):
        rows_x.along_x(k)

    rin = y_lanes(rp_s, y)[...].astype(F32)
    for k in range(1, NY):
        far(y_lanes(rp_s, y), rp_r.at[k], gy_ss.at[k], gy_rs.at[k], y_dev(k)).wait_recv()
        rin = rin + rp_r[k].astype(F32)
    rin = rin.T[0:96, :].astype(BF)

    for load in loads[5:]:
        load.wait()
    sa_row = jnp.concatenate([sa[...].reshape(1, 96), jnp.zeros((1, 32), F32)], axis=1)
    sa_col[...] = jnp.broadcast_to(sa_row, (128, 128)).T[0:96, 0:1]

    def e_block(ref, k, rows=slice(None)):
        return ref.at[rows, pl.ds(pl.multiple_of(q_of(k) * 384, 128), 384)]

    mine = pl.ds(pl.multiple_of(c * 48, 16), 48)
    other = pl.ds(pl.multiple_of((1 - c) * 48, 16), 48)

    @each(NQ, 0)
    def _(k):
        pt[...] = dot(rin, e_block(bg, k)[...])
        keep[k] = pt[mine, :]
        half_s[k] = pt[other, :].astype(BF)
        far(half_s.at[k], half_r.at[k], h_ss.at[k], h_rs.at[k], sib).start()

    @each(NQ)
    def _(k):
        far(half_s.at[k], half_r.at[k], h_ss.at[k], h_rs.at[k], sib).wait_recv()
        rs_s[k] = (keep[k] + half_r[k].astype(F32)).astype(BF)
        far(rs_s.at[k], rs_r.at[k], p_ss.at[k], p_rs.at[k], q_dev(k)).start()

    cols_step(0)

    @each(NY)
    def _(k):
        far(cnt_y.at[y], cnt_y.at[y], n_ss.at[k], n_rs.at[k], y_dev(k)).start()

    far(half_s.at[0], half_r.at[0], h_ss.at[0], h_rs.at[0], sib).wait_recv()
    keep[0] = keep[0] + half_r[0].astype(F32)

    @each(NQ)
    def _(k):
        far(rs_s.at[k], rs_r.at[k], p_ss.at[k], p_rs.at[k], q_dev(k)).wait_recv()
        keep[0] = keep[0] + rs_r[k].astype(F32)

    sg_here = sg[pl.ds(pl.multiple_of(q * 384, 128), 384)].reshape(1, 384)
    denominator = sa_col[mine, :] * sg_here + DAMPING
    sc_own = e_block(sc, 0, mine)
    sc_own[...] = (keep[0] / denominator).astype(BF)

    @each(NQ)
    def _(k):
        far(sc_own, sc_own, s_ss.at[k], s_rs.at[k], q_dev(k)).start()

    far(sc_own, sc_own, sf_ss.at[0], sf_rs.at[0], sib).start()

    cols_step(1)

    @each(NQ)
    def _(k):
        got = e_block(sc, NQ - k, mine)
        far(got, got, s_ss.at[k], s_rs.at[k], q_dev(k)).wait_recv()
        far(got, got, sf_ss.at[k], sf_rs.at[k], sib).start()

    back[...] = jnp.zeros((192, 96), F32)

    @each(NQ, 0)
    def _(k):
        got = e_block(sc, NQ - k, other)
        far(got, got, sf_ss.at[k], sf_rs.at[k], sib).wait_recv()
        back[...] += dot(e_block(bg, NQ - k)[...], e_block(sc, NQ - k)[...], NT)

    boy_own = y_lanes(boy, y)
    boy_own[:, 0:96] = back[...].astype(BF)
    boy_own[:, 96:128] = jnp.zeros((192, 32), BF)

    @each(NY)
    def _(k):
        far(boy_own, boy_own, o_ss.at[k], o_rs.at[k], y_dev(k)).start()

    rows_x.to_core()

    cols_step(2)

    @each(NY)
    def _(k):
        slot = y_lanes(boy, y_of(NY - k))
        far(slot, slot, o_ss.at[k], o_rs.at[k], y_dev(k)).wait_recv()

    def pz_half(h, k):
        rows = pl.ds(96 * h, 96)
        return far(pz_s.at[k, rows, :], pz.at[k, rows, :], z_ss.at[h, k], z_rs.at[h, k], z_dev(k))

    @each(NZ + 1)
    def _(k):
        to = z_of(k)
        rows = r_ba[pl.ds(pl.multiple_of(to * 128, 128), 128), :]
        pz_s[k] = dot(boy[...], rows, NT).astype(BF)

        @pl.when(k < NZ)
        def _():
            pz_half(0, k).start()

    each(NZ)(lambda k: pz_half(1, k).start())

    rows_x.arrive()

    @each(NY)
    def _(k):
        tile = cnt_y.at[y_of(NY - k)]
        far(tile, tile, n_ss.at[k], n_rs.at[k], y_dev(k)).wait_recv()

    cols_step(3)
    for lo in (0, 256):
        for i in range(NY):
            rows = r_buf[i, :, :, lo : lo + 256].reshape(768, 256)
            term = dot(rows, c_buf[i, :, lo : lo + 256], NT)
            acc[:, lo : lo + 192] = term if i == 0 else acc[:, lo : lo + 192] + term
    cnt_s[...] = cnt_y[0] + cnt_y[1] + cnt_y[2] + cnt_y[3]

    @each(NZ, 0)
    def _(k):
        to = z_of(k)
        rows = pl.ds(pl.multiple_of(to * 96, 32), 96)
        az_s[k] = jnp.concatenate([acc[rows, 0:192], acc[rows, 256:448]], axis=1).astype(BF)

        @pl.when(k > 0)
        def _():
            far(az_s.at[k], az.at[k], a_ss.at[k], a_rs.at[k], z_dev(k)).start()
            far(cnt_s, cnt_z.at[k], m_ss.at[k], m_rs.at[k], z_dev(k)).start()

    def py_half(h, k):
        slot = py.at[y, pl.ds(96 * h, 96), :]
        return far(slot, slot, q_ss.at[h, k], q_rs.at[h, k], y_dev(k))

    for h in range(2):
        rows = slice(96 * h, 96 * h + 96)
        total = pz_s[NZ, rows, :].astype(F32)
        for k in range(1, NZ):
            pz_half(h, k).wait_recv()
            total = total + pz[k, rows, :].astype(F32)
        py[y, rows, :] = total.astype(BF)
        each(NY)(lambda k: py_half(h, k).start())

    def finish_factors():
        @each(NZ)
        def _(k):
            far(az_s.at[k], az.at[k], a_ss.at[k], a_rs.at[k], z_dev(k)).wait_recv()
            far(cnt_s, cnt_z.at[k], m_ss.at[k], m_rs.at[k], z_dev(k)).wait_recv()

        stat = az_s[0].astype(F32)
        count = cnt_s[...]
        for k in range(1, NZ):
            stat = stat + az[k].astype(F32)
            count = count + cnt_z[k]
        scale = (1.0 - DECAY) / count[0:1, 0:1]
        fa_new[...] = DECAY * fa_old[...] + stat[:, 0:192] * scale
        fg_new[...] = DECAY * fg_old[...] + stat[:, 192:384] * scale

    def ring_copy(h, way, k, arriving):
        at = z_of((NZ - 1, 1)[way] * (k + arriving))
        lo, n = (96 * h, 96) if k < 3 else (96 * h + 48 * way, 48)
        slot = out.at[pl.ds(lo, n), pl.ds(pl.multiple_of(at * 384, 128), 384)]
        return far(slot, slot, f_ss.at[h, way, k], f_rs.at[h, way, k], z_dev((1, NZ - 1)[way]))

    for k in range(5):
        for h in range(2):
            if k == 0:
                rows = pl.ds(96 * h, 96)
                for j in range(1, NY):
                    py_half(h, j).wait_recv()
                out[rows, pl.ds(pl.multiple_of(z * 384, 128), 384)] = lanes4(
                    [py[i, 96 * h : 96 * h + 96, 0:96] for i in range(NY)]
                )
            for way in range(2):
                if k > 0:
                    ring_copy(h, way, k - 1, 1).wait_recv()
                if k < 4:
                    ring_copy(h, way, k, 0).start()
        if k == 3:
            finish_factors()

    @each(NY)
    def _(k):
        far(y_lanes(rp_s, y), rp_r.at[k], gy_ss.at[k], gy_rs.at[k], y_dev(k)).wait_send()
        far(cnt_y.at[y], cnt_y.at[y], n_ss.at[k], n_rs.at[k], y_dev(k)).wait_send()
        far(boy_own, boy_own, o_ss.at[k], o_rs.at[k], y_dev(k)).wait_send()
        py_half(0, k).wait_send()
        py_half(1, k).wait_send()

    @each(NQ)
    def _(k):
        far(rs_s.at[k], rs_r.at[k], p_ss.at[k], p_rs.at[k], q_dev(k)).wait_send()
        far(sc_own, sc_own, s_ss.at[k], s_rs.at[k], q_dev(k)).wait_send()
        far(g_own, g_own, g_ss.at[k], g_rs.at[k], z_dev(k)).wait_send()
        far(az_s.at[k], az.at[k], a_ss.at[k], a_rs.at[k], z_dev(k)).wait_send()
        far(cnt_s, cnt_z.at[k], m_ss.at[k], m_rs.at[k], z_dev(k)).wait_send()
        pz_half(0, k).wait_send()
        pz_half(1, k).wait_send()

    @each(NQ, 0)
    def _(k):
        far(half_s.at[k], half_r.at[k], h_ss.at[k], h_rs.at[k], sib).wait_send()
        far(sc_own, sc_own, sf_ss.at[k], sf_rs.at[k], sib).wait_send()

    for d in range(NY - 1):
        for ok, onward, copy in cols_copies(d):
            pl.when(onward)(copy.wait_send)

    rows_b.sent()
    rows_x.sent()

    for h in range(2):
        for way in range(2):
            for k in range(4):
                ring_copy(h, way, k, 0).wait_send()


def local(
    layer_inputs,
    output_cotangents,
    valid,
    factor_a_old,
    factor_g_old,
    weight_gradient,
    basis_g,
    basis_a,
    spectrum_g,
    spectrum_a,
):
    V = pltpu.VMEM
    dma = pltpu.SemaphoreType.DMA
    scratch = [
        V((192, 256), BF), V((192, 256), BF), V((256,), jnp.int32),
        V((96, 192), F32), V((96, 192), F32), V((192, 96), BF),
        V((192, 3072), BF), V((192, 96), BF), V((3072,), F32), V((96,), F32), dma((10,)),
        V((96, 1), F32),
        V((192, 512), BF),
        V((4, 8, 96, 512), BF),
        V((4, 192, 512), BF),
        V((192, 128), BF),
        V((1024, 512), BF),
        V((768, 512), F32),
        V((8, 96, 384), BF),
        V((8, 96, 384), BF),
        V((4, 8, 128), F32),
        V((8, 128), F32),
        V((8, 8, 128), F32),
        V((192, 1024), BF),
        V((192, 512), BF),
        V((4, 192, 128), BF),
        V((96, 384), F32),
        V((8, 48, 384), BF),
        V((8, 48, 384), BF),
        V((8, 48, 384), F32),
        V((8, 48, 384), BF),
        V((8, 48, 384), BF),
        V((96, 3072), BF),
        V((192, 96), F32),
        V((192, 512), BF),
        V((9, 192, 128), BF),
        V((8, 192, 128), BF),
        V((4, 192, 128), BF),
        dma((4,)), dma((4,)),
        dma((8,)), dma((8,)), dma((2, 2, 4)), dma((2, 2, 4)),
        dma((4,)), dma((4, 4)), dma((4, 4)), dma((4, 8)),
        dma((4,)), dma((4, 4)), dma((4, 4)), dma((4, 8)),
        dma((2, 4)), dma((4,)), dma((4,)), dma((4,)), dma((8,)), dma((8,)),
        dma((8,)), dma((8,)), dma((8,)), dma((8,)), dma((8,)), dma((8,)), dma((8,)), dma((8,)),
        dma((8,)), dma((8,)), dma((4,)), dma((4,)), dma((2, 8)), dma((2, 8)), dma((2, 4)), dma((2, 4)),
    ]
    return pl.pallas_call(
        kernel,
        out_shape=(V((96, 192), F32), V((96, 192), F32), V((192, 3072), BF)),
        in_specs=[pl.BlockSpec(memory_space=pltpu.HBM)] * 10,
        out_specs=(pl.BlockSpec(memory_space=V),) * 3,
        scratch_shapes=scratch,
        compiler_params=pltpu.CompilerParams(
            collective_id=0, has_side_effects=True, vmem_limit_bytes=62 * 1024 * 1024
        ),
    )(
        layer_inputs.T,
        output_cotangents.T,
        valid,
        factor_a_old,
        factor_g_old,
        weight_gradient,
        basis_g,
        basis_a,
        spectrum_g,
        spectrum_a,
    )


def solution(mesh):
    placed = (
        P("rep", "shard"),
        P("rep", "shard"),
        P("rep"),
        P("rep", "shard"),
        P("rep", "shard"),
        P("shard", "rep"),
        P("shard", None),
        P("shard", "rep"),
        P(),
        P("rep"),
    )
    return jax.shard_map(
        local,
        mesh=mesh,
        in_specs=placed,
        out_specs=(P("rep", "shard"), P("rep", "shard"), P("shard", None)),
        check_vma=False,
    )
```

```python
import jax
import jax.numpy as jnp
from jax import lax
from jax.experimental import pallas as pl
from jax.experimental.pallas import tpu as pltpu
from jax.sharding import PartitionSpec as P

DAMPING = 0.03
DECAY = 0.95

NZ, NY, NQ, NX = 8, 4, 8, 4
BF, F32 = jnp.bfloat16, jnp.float32
NT = (((1,), (1,)), ((), ()))


def dot(a, b, dims=(((1,), (0,)), ((), ()))):
    return lax.dot_general(a, b, dims, preferred_element_type=F32)


def lanes4(parts):
    return jnp.concatenate([p.astype(F32) for p in parts], axis=1).astype(BF)


def kernel(
    xa_in, xg_in, valid_in, fa_in, fg_in, grad_in, bg_in, ba_in, sg_in, sa_in,
    fa_new, fg_new, out,
    xa, xg, valid, fa_old, fg_old, grad, bg, ba, sg, sa, in_sems, sa_col,
    d_buf, r_buf, c_buf, b_buf, r_ba, acc, az_s, az, cnt_y, cnt_s, cnt_z,
    gz, rp_s, rp_r, pt, half_s, half_r, keep, rs_s, rs_r, sc,
    back, boy, pz_s, pz, py,
    gy_ss, gy_rs, g_ss, g_rs, f_ss, f_rs, rb1_ss, rb2_ss, rb3_ss, rb1_rs, rb2_rs, rb3_rs,
    r1_ss, r2_ss, r3_ss, r1_rs, r2_rs, r3_rs, c_ss, c_rs, n_ss, n_rs, m_ss, m_rs,
    h_ss, h_rs, p_ss, p_rs, s_ss, s_rs, sf_ss, sf_rs,
    a_ss, a_rs, o_ss, o_rs, z_ss, z_rs, q_ss, q_rs,
):
    r = lax.axis_index("rep")
    s = lax.axis_index("shard")
    z, y = lax.div(r, NY), lax.rem(r, NY)
    q, c = lax.div(s, 2), lax.rem(s, 2)
    yh, x = lax.div(q, NX), lax.rem(q, NX)
    half = lax.div(y, 2)

    def y_of(k):
        return lax.rem(y + k, NY)

    def z_of(k):
        return lax.rem(z + k, NZ)

    def q_of(k):
        return lax.rem(q + k, NQ)

    def y_dev(k):
        return (z * NY + y_of(k), s)

    def z_dev(k):
        return (z_of(k) * NY + y, s)

    def q_dev(k):
        return (r, q_of(k) * 2 + c)

    def x_dev(k):
        return (r, (yh * NX + lax.rem(x + k, NX)) * 2 + c)

    sib = (r, q * 2 + 1 - c)

    def far(src, dst, ss, rs, dev):
        return pltpu.make_async_remote_copy(
            src_ref=src, dst_ref=dst, send_sem=ss, recv_sem=rs,
            device_id=dev, device_id_type=pl.DeviceIdType.MESH,
        )

    def each(n, first=1):
        def deco(body):
            def step(k, carry):
                body(k)
                return carry
            lax.fori_loop(first, n, step, 0)
        return deco

    loads = [
        pltpu.make_async_copy(src, dst, in_sems.at[i])
        for i, (src, dst) in enumerate((
            (grad_in, grad), (ba_in, ba), (xa_in, xa), (xg_in, xg), (valid_in, valid),
            (bg_in, bg), (sg_in, sg), (sa_in, sa), (fa_in, fa_old), (fg_in, fg_old),
        ))
    ]
    for load in loads:
        load.start()

    gate = pltpu.get_barrier_semaphore()

    def greet(dev):
        pl.semaphore_signal(gate, inc=1, device_id=dev, device_id_type=pl.DeviceIdType.MESH)

    each(NY)(lambda k: greet(y_dev(k)))
    each(NZ)(lambda k: greet(z_dev(k)))
    each(NQ)(lambda k: greet(q_dev(k)))
    greet(sib)
    own_piece = jnp.logical_and(half == c, yh == c)

    @each(NY, 0)
    def _(j):
        itself = jnp.logical_and(own_piece, j == y)

        @pl.when(jnp.logical_not(itself))
        def _():
            greet((z * NY + j, (c * NX + x) * 2 + half))

    c_own = c_buf.at[y]
    b_own = b_buf
    for load in loads[:5]:
        load.wait()
    g_own = gz.at[:, pl.ds(pl.multiple_of(z * 128, 128), 128)]
    g_own[:, 0:96] = grad[...]
    g_own[:, 96:128] = jnp.zeros((192, 32), BF)
    b_own[:, 0:96] = ba[...]
    b_own[:, 96:128] = jnp.zeros((192, 32), BF)
    for i in range(NQ):
        r_ba[128 * i + 96 : 128 * i + 128, :] = jnp.zeros((32, 512), BF)
    m = valid[...].reshape(1, 256).astype(F32)
    d_buf[:, 0:256] = xa[...]
    d_buf[:, 256:512] = xg[...]

    pl.semaphore_wait(gate, 3 + 7 + 7 + 1 + 4 - jnp.where(own_piece, 1, 0))

    class Plane:
        def __init__(self, src, slot, column, ss1, ss2, ss3, rs1, rs2, rs3):
            self.src, self.slot, self.column = src, slot, column
            self.ss1, self.ss2, self.ss3 = ss1, ss2, ss3
            self.rs1, self.rs2, self.rs3 = rs1, rs2, rs3

        def piece(self, h, t):
            dev = (z * NY + 2 * c + h, (t * NX + x) * 2 + yh)
            itself = jnp.logical_and(dev[0] == r, dev[1] == s)
            src, dst = self.src.at[pl.ds(96 * h, 96), :], self.slot(y, q)
            return itself, src, dst, far(src, dst, self.ss1.at[2 * h + t], self.rs1.at[y], dev)

        def along_y(self):
            for h in range(2):
                for t in range(2):
                    itself, src, dst, copy = self.piece(h, t)

                    @pl.when(jnp.logical_not(itself))
                    def _():
                        copy.start()

                    @pl.when(itself)
                    def _():
                        pltpu.make_async_copy(src, dst, self.rs1.at[y]).start()

        def x_copy(self, j, back):
            block = self.column(c * NX + lax.rem(x + NX - back, NX))
            return far(block, block, self.ss2.at[j], self.rs2.at[j], x_dev(j))

        def core_copy(self, j, core):
            block = self.column(core * NX + lax.rem(x + NX - j, NX))
            return far(block, block, self.ss3.at[j], self.rs3.at[j], sib)

        def along_x(self):
            @each(NY, 0)
            def _(k):
                slot = self.slot(k, c * NX + x)
                far(slot, slot, self.ss1.at[0], self.rs1.at[k], sib).wait_recv()

            each(NX)(lambda j: self.x_copy(j, 0).start())
            self.core_copy(0, c).start()

        def to_core(self):
            @each(NX)
            def _(j):
                self.x_copy(j, j).wait_recv()
                self.core_copy(j, c).start()

        def arrive(self):
            each(NX, 0)(lambda j: self.core_copy(j, 1 - c).wait_recv())

        def sent(self):
            for h in range(2):
                for t in range(2):
                    itself, src, dst, copy = self.piece(h, t)

                    @pl.when(jnp.logical_not(itself))
                    def _():
                        copy.wait_send()

            each(NX)(lambda j: self.x_copy(j, 0).wait_send())
            each(NX, 0)(lambda j: self.core_copy(j, c).wait_send())

    def ba_slot(k, col):
        return r_ba.at[pl.ds(pl.multiple_of(col * 128, 128), 96), pl.ds(pl.multiple_of(k * 128, 128), 128)]

    def ba_column(col):
        return r_ba.at[pl.ds(pl.multiple_of(col * 128, 128), 96), :]

    rows_b = Plane(b_own, ba_slot, ba_column, rb1_ss, rb2_ss, rb3_ss, rb1_rs, rb2_rs, rb3_rs)
    rows_x = Plane(
        d_buf, lambda k, col: r_buf.at[col, k], lambda col: r_buf.at[col],
        r1_ss, r2_ss, r3_ss, r1_rs, r2_rs, r3_rs,
    )

    @each(NZ)
    def _(k):
        far(g_own, g_own, g_ss.at[k], g_rs.at[k], z_dev(k)).start()

    rows_b.along_y()
    c_own[:, 0:256] = (xa[...].astype(F32) * m).astype(BF)
    c_own[:, 256:512] = (xg[...].astype(F32) * m).astype(BF)
    cnt_y[y] = jnp.broadcast_to(jnp.sum(m, axis=1, keepdims=True), (8, 128))
    rows_b.along_x()
    rows_x.along_y()
    rows_b.to_core()
    rows_b.arrive()

    @each(NZ)
    def _(k):
        got = gz.at[:, pl.ds(pl.multiple_of(z_of(NZ - k) * 128, 128), 128)]
        far(got, got, g_ss.at[k], g_rs.at[k], z_dev(k)).wait_recv()

    def cols_copies(d):
        for way, sign, ok, end in ((0, -1, y >= d, y < NY - 1), (1, 1, y + d < NY, y > 0)):
            slot = c_buf.at[jnp.clip(y + sign * d, 0, NY - 1)]
            who = jnp.clip(y + sign * d, 0, NY - 1)
            to = (jnp.clip(y - sign, 0, NY - 1) + z * NY, s)
            yield ok, jnp.logical_and(ok, end), far(slot, slot, c_ss.at[way, d], c_rs.at[who], to)

    def cols_step(d):
        for ok, onward, copy in cols_copies(d):
            if d > 0:
                pl.when(ok)(copy.wait_recv)
            if d < NY - 1:
                pl.when(onward)(copy.start)

    def y_lanes(ref, i):
        return ref.at[:, pl.ds(pl.multiple_of(i * 128, 128), 128)]

    @each(NY + 1)
    def _(k):
        to = y_of(k)
        y_lanes(rp_s, to)[...] = dot(gz[...], y_lanes(r_ba, to)[...]).astype(BF)

        @pl.when(k < NY)
        def _():
            far(y_lanes(rp_s, to), rp_r.at[k], gy_ss.at[k], gy_rs.at[k], y_dev(k)).start()

    rows_x.along_x()

    rin = y_lanes(rp_s, y)[...].astype(F32)
    for k in range(1, NY):
        far(y_lanes(rp_s, y), rp_r.at[k], gy_ss.at[k], gy_rs.at[k], y_dev(k)).wait_recv()
        rin = rin + rp_r[k].astype(F32)
    rin = rin.T[0:96, :].astype(BF)

    for load in loads[5:]:
        load.wait()
    sa_row = jnp.concatenate([sa[...].reshape(1, 96), jnp.zeros((1, 32), F32)], axis=1)
    sa_col[...] = jnp.broadcast_to(sa_row, (128, 128)).T[0:96, 0:1]

    def e_block(ref, k, rows=slice(None)):
        return ref.at[rows, pl.ds(pl.multiple_of(q_of(k) * 384, 128), 384)]

    mine = pl.ds(pl.multiple_of(c * 48, 16), 48)
    other = pl.ds(pl.multiple_of((1 - c) * 48, 16), 48)

    @each(NQ, 0)
    def _(k):
        pt[...] = dot(rin, e_block(bg, k)[...])
        keep[k] = pt[mine, :]
        half_s[k] = pt[other, :].astype(BF)
        far(half_s.at[k], half_r.at[k], h_ss.at[k], h_rs.at[k], sib).start()

    @each(NQ)
    def _(k):
        far(half_s.at[k], half_r.at[k], h_ss.at[k], h_rs.at[k], sib).wait_recv()
        rs_s[k] = (keep[k] + half_r[k].astype(F32)).astype(BF)
        far(rs_s.at[k], rs_r.at[k], p_ss.at[k], p_rs.at[k], q_dev(k)).start()

    cols_step(0)

    @each(NY)
    def _(k):
        far(cnt_y.at[y], cnt_y.at[y], n_ss.at[k], n_rs.at[k], y_dev(k)).start()

    far(half_s.at[0], half_r.at[0], h_ss.at[0], h_rs.at[0], sib).wait_recv()
    keep[0] = keep[0] + half_r[0].astype(F32)

    @each(NQ)
    def _(k):
        far(rs_s.at[k], rs_r.at[k], p_ss.at[k], p_rs.at[k], q_dev(k)).wait_recv()
        keep[0] = keep[0] + rs_r[k].astype(F32)

    sg_here = sg[pl.ds(pl.multiple_of(q * 384, 128), 384)].reshape(1, 384)
    denominator = sa_col[mine, :] * sg_here + DAMPING
    sc_own = e_block(sc, 0, mine)
    sc_own[...] = (keep[0] / denominator).astype(BF)

    @each(NQ)
    def _(k):
        far(sc_own, sc_own, s_ss.at[k], s_rs.at[k], q_dev(k)).start()

    far(sc_own, sc_own, sf_ss.at[0], sf_rs.at[0], sib).start()

    cols_step(1)

    @each(NQ)
    def _(k):
        got = e_block(sc, NQ - k, mine)
        far(got, got, s_ss.at[k], s_rs.at[k], q_dev(k)).wait_recv()
        far(got, got, sf_ss.at[k], sf_rs.at[k], sib).start()

    back[...] = jnp.zeros((192, 96), F32)

    @each(NQ, 0)
    def _(k):
        got = e_block(sc, NQ - k, other)
        far(got, got, sf_ss.at[k], sf_rs.at[k], sib).wait_recv()
        back[...] += dot(e_block(bg, NQ - k)[...], e_block(sc, NQ - k)[...], NT)

    boy_own = y_lanes(boy, y)
    boy_own[:, 0:96] = back[...].astype(BF)
    boy_own[:, 96:128] = jnp.zeros((192, 32), BF)

    @each(NY)
    def _(k):
        far(boy_own, boy_own, o_ss.at[k], o_rs.at[k], y_dev(k)).start()

    rows_x.to_core()

    cols_step(2)

    @each(NY)
    def _(k):
        slot = y_lanes(boy, y_of(NY - k))
        far(slot, slot, o_ss.at[k], o_rs.at[k], y_dev(k)).wait_recv()

    def pz_half(h, k):
        rows = pl.ds(96 * h, 96)
        return far(pz_s.at[k, rows, :], pz.at[k, rows, :], z_ss.at[h, k], z_rs.at[h, k], z_dev(k))

    @each(NZ + 1)
    def _(k):
        to = z_of(k)
        rows = r_ba[pl.ds(pl.multiple_of(to * 128, 128), 128), :]
        pz_s[k] = dot(boy[...], rows, NT).astype(BF)

        @pl.when(k < NZ)
        def _():
            pz_half(0, k).start()

    each(NZ)(lambda k: pz_half(1, k).start())

    rows_x.arrive()

    @each(NY)
    def _(k):
        tile = cnt_y.at[y_of(NY - k)]
        far(tile, tile, n_ss.at[k], n_rs.at[k], y_dev(k)).wait_recv()

    cols_step(3)
    for lo in (0, 256):
        for i in range(NY):
            rows = r_buf[:, i, :, lo : lo + 256].reshape(768, 256)
            term = dot(rows, c_buf[i, :, lo : lo + 256], NT)
            acc[:, lo : lo + 192] = term if i == 0 else acc[:, lo : lo + 192] + term
    cnt_s[...] = cnt_y[0] + cnt_y[1] + cnt_y[2] + cnt_y[3]

    @each(NZ, 0)
    def _(k):
        to = z_of(k)
        rows = pl.ds(pl.multiple_of(to * 96, 32), 96)
        az_s[k] = jnp.concatenate([acc[rows, 0:192], acc[rows, 256:448]], axis=1).astype(BF)

        @pl.when(k > 0)
        def _():
            far(cnt_s, cnt_z.at[k], m_ss.at[k], m_rs.at[k], z_dev(k)).start()

    def sum_rows(way, k):
        return pl.ds(48 * way, 48) if k == 0 else pl.ds(0, 96)

    def sum_copy(way, k):
        rows = sum_rows(way, k)
        return far(az_s.at[(4 - k, 4 + k)[way], rows, :], az.at[way, k, rows, :],
                   a_ss.at[way, k], a_rs.at[way, k], z_dev((1, NZ - 1)[way]))

    def sum_step(k):
        for way in range(2):
            if k > 0:
                sum_copy(way, k - 1).wait_recv()
                rows, at = sum_rows(way, k - 1), (4 - k, 4 + k)[way]
                az_s[at, rows, :] = (az_s[at, rows, :].astype(F32) + az[way, k - 1, rows, :].astype(F32)).astype(BF)
            sum_copy(way, k).start()

    sum_step(0)

    def py_half(h, k):
        slot = py.at[y, pl.ds(96 * h, 96), :]
        return far(slot, slot, q_ss.at[h, k], q_rs.at[h, k], y_dev(k))

    for h in range(2):
        rows = slice(96 * h, 96 * h + 96)
        total = pz_s[NZ, rows, :].astype(F32)
        for k in range(1, NZ):
            pz_half(h, k).wait_recv()
            total = total + pz[k, rows, :].astype(F32)
        py[y, rows, :] = total.astype(BF)
        each(NY)(lambda k: py_half(h, k).start())

    def finish_factors():
        @each(NZ)
        def _(k):
            far(cnt_s, cnt_z.at[k], m_ss.at[k], m_rs.at[k], z_dev(k)).wait_recv()

        for way in range(2):
            sum_copy(way, 3).wait_recv()
        stat = az_s[0].astype(F32) + az[0, 3].astype(F32) + az[1, 3].astype(F32)
        count = cnt_s[...]
        for k in range(1, NZ):
            count = count + cnt_z[k]
        scale = (1.0 - DECAY) / count[0:1, 0:1]
        fa_new[...] = DECAY * fa_old[...] + stat[:, 0:192] * scale
        fg_new[...] = DECAY * fg_old[...] + stat[:, 192:384] * scale

    sum_step(1)

    def ring_copy(h, way, k, arriving):
        at = z_of((NZ - 1, 1)[way] * (k + arriving))
        lo, n = (96 * h, 96) if k < 3 else (96 * h + 48 * way, 48)
        slot = out.at[pl.ds(lo, n), pl.ds(pl.multiple_of(at * 384, 128), 384)]
        return far(slot, slot, f_ss.at[h, way, k], f_rs.at[h, way, k], z_dev((1, NZ - 1)[way]))

    for k in range(5):
        for h in range(2):
            if k == 0:
                rows = pl.ds(96 * h, 96)
                for j in range(1, NY):
                    py_half(h, j).wait_recv()
                out[rows, pl.ds(pl.multiple_of(z * 384, 128), 384)] = lanes4(
                    [py[i, 96 * h : 96 * h + 96, 0:96] for i in range(NY)]
                )
            for way in range(2):
                if k > 0:
                    ring_copy(h, way, k - 1, 1).wait_recv()
                if k < 4:
                    ring_copy(h, way, k, 0).start()
        if k == 0:
            sum_step(2)
        if k == 1:
            sum_step(3)
        if k == 3:
            finish_factors()

    @each(NY)
    def _(k):
        far(y_lanes(rp_s, y), rp_r.at[k], gy_ss.at[k], gy_rs.at[k], y_dev(k)).wait_send()
        far(cnt_y.at[y], cnt_y.at[y], n_ss.at[k], n_rs.at[k], y_dev(k)).wait_send()
        far(boy_own, boy_own, o_ss.at[k], o_rs.at[k], y_dev(k)).wait_send()
        py_half(0, k).wait_send()
        py_half(1, k).wait_send()

    @each(NQ)
    def _(k):
        far(rs_s.at[k], rs_r.at[k], p_ss.at[k], p_rs.at[k], q_dev(k)).wait_send()
        far(sc_own, sc_own, s_ss.at[k], s_rs.at[k], q_dev(k)).wait_send()
        far(g_own, g_own, g_ss.at[k], g_rs.at[k], z_dev(k)).wait_send()
        far(cnt_s, cnt_z.at[k], m_ss.at[k], m_rs.at[k], z_dev(k)).wait_send()
        pz_half(0, k).wait_send()
        pz_half(1, k).wait_send()

    @each(NQ, 0)
    def _(k):
        far(half_s.at[k], half_r.at[k], h_ss.at[k], h_rs.at[k], sib).wait_send()
        far(sc_own, sc_own, sf_ss.at[k], sf_rs.at[k], sib).wait_send()

    for d in range(NY - 1):
        for ok, onward, copy in cols_copies(d):
            pl.when(onward)(copy.wait_send)

    for k in range(4):
        for way in range(2):
            sum_copy(way, k).wait_send()

    rows_b.sent()
    rows_x.sent()

    for h in range(2):
        for way in range(2):
            for k in range(4):
                ring_copy(h, way, k, 0).wait_send()


def local(
    layer_inputs,
    output_cotangents,
    valid,
    factor_a_old,
    factor_g_old,
    weight_gradient,
    basis_g,
    basis_a,
    spectrum_g,
    spectrum_a,
):
    V = pltpu.VMEM
    dma = pltpu.SemaphoreType.DMA
    scratch = [
        V((192, 256), BF), V((192, 256), BF), V((256,), jnp.int32),
        V((96, 192), F32), V((96, 192), F32), V((192, 96), BF),
        V((192, 3072), BF), V((192, 96), BF), V((3072,), F32), V((96,), F32), dma((10,)),
        V((96, 1), F32),
        V((192, 512), BF),
        V((8, 4, 96, 512), BF),
        V((4, 192, 512), BF),
        V((192, 128), BF),
        V((1024, 512), BF),
        V((768, 512), F32),
        V((8, 96, 384), BF),
        V((2, 4, 96, 384), BF),
        V((4, 8, 128), F32),
        V((8, 128), F32),
        V((8, 8, 128), F32),
        V((192, 1024), BF),
        V((192, 512), BF),
        V((4, 192, 128), BF),
        V((96, 384), F32),
        V((8, 48, 384), BF),
        V((8, 48, 384), BF),
        V((8, 48, 384), F32),
        V((8, 48, 384), BF),
        V((8, 48, 384), BF),
        V((96, 3072), BF),
        V((192, 96), F32),
        V((192, 512), BF),
        V((9, 192, 128), BF),
        V((8, 192, 128), BF),
        V((4, 192, 128), BF),
        dma((4,)), dma((4,)),
        dma((8,)), dma((8,)), dma((2, 2, 4)), dma((2, 2, 4)),
        *[dma((4,))] * 6,
        *[dma((4,))] * 6,
        dma((2, 4)), dma((4,)), dma((4,)), dma((4,)), dma((8,)), dma((8,)),
        dma((8,)), dma((8,)), dma((8,)), dma((8,)), dma((8,)), dma((8,)), dma((8,)), dma((8,)),
        dma((2, 4)), dma((2, 4)), dma((4,)), dma((4,)), dma((2, 8)), dma((2, 8)), dma((2, 4)), dma((2, 4)),
    ]
    return pl.pallas_call(
        kernel,
        out_shape=(V((96, 192), F32), V((96, 192), F32), V((192, 3072), BF)),
        in_specs=[pl.BlockSpec(memory_space=pltpu.HBM)] * 10,
        out_specs=(pl.BlockSpec(memory_space=V),) * 3,
        scratch_shapes=scratch,
        compiler_params=pltpu.CompilerParams(
            collective_id=0, has_side_effects=True, vmem_limit_bytes=62 * 1024 * 1024
        ),
    )(
        layer_inputs.T,
        output_cotangents.T,
        valid,
        factor_a_old,
        factor_g_old,
        weight_gradient,
        basis_g,
        basis_a,
        spectrum_g,
        spectrum_a,
    )


def solution(mesh):
    placed = (
        P("rep", "shard"),
        P("rep", "shard"),
        P("rep"),
        P("rep", "shard"),
        P("rep", "shard"),
        P("shard", "rep"),
        P("shard", None),
        P("shard", "rep"),
        P(),
        P("rep"),
    )
    return jax.shard_map(
        local,
        mesh=mesh,
        in_specs=placed,
        out_specs=(P("rep", "shard"), P("rep", "shard"), P("shard", None)),
        check_vma=False,
    )
```

```python
import jax
import jax.numpy as jnp
from jax import lax
from jax.experimental import pallas as pl
from jax.experimental.pallas import tpu as pltpu
from jax.sharding import PartitionSpec as P

DAMPING = 0.03
DECAY = 0.95

NZ, NY, NQ, NX = 8, 4, 8, 4
BF, F32 = jnp.bfloat16, jnp.float32
NT = (((1,), (1,)), ((), ()))


def dot(a, b, dims=(((1,), (0,)), ((), ()))):
    return lax.dot_general(a, b, dims, preferred_element_type=F32)


def lanes4(parts):
    return jnp.concatenate([p.astype(F32) for p in parts], axis=1).astype(BF)


def kernel(
    xa_in, xg_in, valid_in, fa_in, fg_in, grad_in, bg_in, ba_in, sg_in, sa_in,
    fa_new, fg_new, out,
    xa, xg, valid, fa_old, fg_old, grad, bg, ba, sg, sa, in_sems, sa_col,
    d_buf, r_buf, c_buf, b_buf, r_ba, acc, az_s, az, cnt_y, cnt_s, cnt_z,
    gz, rp_s, rp_r, pt, half_s, half_r, keep, rs_s, rs_r, sc,
    back, boy, pz_s, pz, py,
    gy_ss, gy_rs, g_ss, g_rs, f_ss, f_rs, rb1_ss, rb2_ss, rb3_ss, rb1_rs, rb2_rs, rb3_rs,
    r1_ss, r2_ss, r3_ss, r1_rs, r2_rs, r3_rs, c_ss, c_rs, n_ss, n_rs, m_ss, m_rs,
    h_ss, h_rs, p_ss, p_rs, s_ss, s_rs, sf_ss, sf_rs,
    a_ss, a_rs, o_ss, o_rs, z_ss, z_rs, q_ss, q_rs,
):
    r = lax.axis_index("rep")
    s = lax.axis_index("shard")
    z, y = lax.div(r, NY), lax.rem(r, NY)
    q, c = lax.div(s, 2), lax.rem(s, 2)
    yh, x = lax.div(q, NX), lax.rem(q, NX)
    half = lax.div(y, 2)

    def y_of(k):
        return lax.rem(y + k, NY)

    def z_of(k):
        return lax.rem(z + k, NZ)

    def q_of(k):
        return lax.rem(yh + k // NX, 2) * NX + lax.rem(x + k % NX, NX)

    def q_from(k):
        return lax.rem(yh + k // NX, 2) * NX + lax.rem(x + NX - k % NX, NX)

    def y_dev(k):
        return (z * NY + y_of(k), s)

    def z_dev(k):
        return (z_of(k) * NY + y, s)

    def q_dev(k):
        return (r, q_of(k) * 2 + c)

    def x_dev(k):
        return (r, (yh * NX + lax.rem(x + k, NX)) * 2 + c)

    sib = (r, q * 2 + 1 - c)

    def far(src, dst, ss, rs, dev):
        return pltpu.make_async_remote_copy(
            src_ref=src, dst_ref=dst, send_sem=ss, recv_sem=rs,
            device_id=dev, device_id_type=pl.DeviceIdType.MESH,
        )

    def each(n, first=1):
        def deco(body):
            def step(k, carry):
                body(k)
                return carry
            lax.fori_loop(first, n, step, 0)
        return deco

    loads = [
        pltpu.make_async_copy(src, dst, in_sems.at[i])
        for i, (src, dst) in enumerate((
            (grad_in, grad), (ba_in, ba), (xa_in, xa), (xg_in, xg), (valid_in, valid),
            (bg_in, bg), (sg_in, sg), (sa_in, sa), (fa_in, fa_old), (fg_in, fg_old),
        ))
    ]
    for load in loads:
        load.start()

    gate = pltpu.get_barrier_semaphore()

    def greet(dev):
        pl.semaphore_signal(gate, inc=1, device_id=dev, device_id_type=pl.DeviceIdType.MESH)

    each(NY)(lambda k: greet(y_dev(k)))
    each(NZ)(lambda k: greet(z_dev(k)))
    each(NQ)(lambda k: greet(q_dev(k)))
    greet(sib)
    own_piece = jnp.logical_and(half == c, yh == c)

    @each(NY, 0)
    def _(j):
        itself = jnp.logical_and(own_piece, j == y)

        @pl.when(jnp.logical_not(itself))
        def _():
            greet((z * NY + j, (c * NX + x) * 2 + half))

    c_own = c_buf.at[y]
    b_own = b_buf
    for load in loads[:5]:
        load.wait()
    g_own = gz.at[:, pl.ds(pl.multiple_of(z * 128, 128), 128)]
    g_own[:, 0:96] = grad[...]
    g_own[:, 96:128] = jnp.zeros((192, 32), BF)
    b_own[:, 0:96] = ba[...]
    b_own[:, 96:128] = jnp.zeros((192, 32), BF)
    for i in range(NQ):
        r_ba[128 * i + 96 : 128 * i + 128, :] = jnp.zeros((32, 512), BF)
    m = valid[...].reshape(1, 256).astype(F32)
    d_buf[:, 0:256] = xa[...]
    d_buf[:, 256:512] = xg[...]

    pl.semaphore_wait(gate, 3 + 7 + 7 + 1 + 4 - jnp.where(own_piece, 1, 0))

    class Plane:
        def __init__(self, src, slot, column, ss1, ss2, ss3, rs1, rs2, rs3):
            self.src, self.slot, self.column = src, slot, column
            self.ss1, self.ss2, self.ss3 = ss1, ss2, ss3
            self.rs1, self.rs2, self.rs3 = rs1, rs2, rs3

        def piece(self, h, t):
            dev = (z * NY + 2 * c + h, (t * NX + x) * 2 + yh)
            itself = jnp.logical_and(dev[0] == r, dev[1] == s)
            src, dst = self.src.at[pl.ds(96 * h, 96), :], self.slot(y, q)
            return itself, src, dst, far(src, dst, self.ss1.at[2 * h + t], self.rs1.at[y], dev)

        def along_y(self):
            for h in range(2):
                for t in range(2):
                    itself, src, dst, copy = self.piece(h, t)

                    @pl.when(jnp.logical_not(itself))
                    def _():
                        copy.start()

                    @pl.when(itself)
                    def _():
                        pltpu.make_async_copy(src, dst, self.rs1.at[y]).start()

        def x_copy(self, j, back):
            block = self.column(c * NX + lax.rem(x + NX - back, NX))
            return far(block, block, self.ss2.at[j], self.rs2.at[j], x_dev(j))

        def core_copy(self, j, core):
            block = self.column(core * NX + lax.rem(x + NX - j, NX))
            return far(block, block, self.ss3.at[j], self.rs3.at[j], sib)

        def along_x(self):
            @each(NY, 0)
            def _(k):
                slot = self.slot(k, c * NX + x)
                far(slot, slot, self.ss1.at[0], self.rs1.at[k], sib).wait_recv()

            each(NX)(lambda j: self.x_copy(j, 0).start())
            self.core_copy(0, c).start()

        def to_core(self):
            @each(NX)
            def _(j):
                self.x_copy(j, j).wait_recv()
                self.core_copy(j, c).start()

        def arrive(self):
            each(NX, 0)(lambda j: self.core_copy(j, 1 - c).wait_recv())

        def sent(self):
            for h in range(2):
                for t in range(2):
                    itself, src, dst, copy = self.piece(h, t)

                    @pl.when(jnp.logical_not(itself))
                    def _():
                        copy.wait_send()

            each(NX)(lambda j: self.x_copy(j, 0).wait_send())
            each(NX, 0)(lambda j: self.core_copy(j, c).wait_send())

    def ba_slot(k, col):
        return r_ba.at[pl.ds(pl.multiple_of(col * 128, 128), 96), pl.ds(pl.multiple_of(k * 128, 128), 128)]

    def ba_column(col):
        return r_ba.at[pl.ds(pl.multiple_of(col * 128, 128), 96), :]

    rows_b = Plane(b_own, ba_slot, ba_column, rb1_ss, rb2_ss, rb3_ss, rb1_rs, rb2_rs, rb3_rs)
    rows_x = Plane(
        d_buf, lambda k, col: r_buf.at[col, k], lambda col: r_buf.at[col],
        r1_ss, r2_ss, r3_ss, r1_rs, r2_rs, r3_rs,
    )

    def opposite_first(j):
        return (j + 2) % 7 + 1

    @each(NZ)
    def _(j):
        k = opposite_first(j)
        far(g_own, g_own, g_ss.at[k], g_rs.at[k], z_dev(k)).start()

    rows_b.along_y()
    c_own[:, 0:256] = (xa[...].astype(F32) * m).astype(BF)
    c_own[:, 256:512] = (xg[...].astype(F32) * m).astype(BF)
    cnt_y[y] = jnp.broadcast_to(jnp.sum(m, axis=1, keepdims=True), (8, 128))
    rows_b.along_x()
    rows_x.along_y()
    rows_b.to_core()
    rows_b.arrive()

    @each(NZ)
    def _(k):
        got = gz.at[:, pl.ds(pl.multiple_of(z_of(NZ - k) * 128, 128), 128)]
        far(got, got, g_ss.at[k], g_rs.at[k], z_dev(k)).wait_recv()

    def cols_copies(d):
        for way, sign, ok, end in ((0, -1, y >= d, y < NY - 1), (1, 1, y + d < NY, y > 0)):
            slot = c_buf.at[jnp.clip(y + sign * d, 0, NY - 1)]
            who = jnp.clip(y + sign * d, 0, NY - 1)
            to = (jnp.clip(y - sign, 0, NY - 1) + z * NY, s)
            yield ok, jnp.logical_and(ok, end), far(slot, slot, c_ss.at[way, d], c_rs.at[who], to)

    def cols_step(d):
        for ok, onward, copy in cols_copies(d):
            if d > 0:
                pl.when(ok)(copy.wait_recv)
            if d < NY - 1:
                pl.when(onward)(copy.start)

    def y_lanes(ref, i):
        return ref.at[:, pl.ds(pl.multiple_of(i * 128, 128), 128)]

    @each(NY + 1)
    def _(k):
        to = y_of(k)
        y_lanes(rp_s, to)[...] = dot(gz[...], y_lanes(r_ba, to)[...]).astype(BF)

        @pl.when(k < NY)
        def _():
            far(y_lanes(rp_s, to), rp_r.at[k], gy_ss.at[k], gy_rs.at[k], y_dev(k)).start()

    rows_x.along_x()

    rin = y_lanes(rp_s, y)[...].astype(F32)
    for k in range(1, NY):
        far(y_lanes(rp_s, y), rp_r.at[k], gy_ss.at[k], gy_rs.at[k], y_dev(k)).wait_recv()
        rin = rin + rp_r[k].astype(F32)
    rin = rin.T[0:96, :].astype(BF)

    for load in loads[5:]:
        load.wait()
    sa_row = jnp.concatenate([sa[...].reshape(1, 96), jnp.zeros((1, 32), F32)], axis=1)
    sa_col[...] = jnp.broadcast_to(sa_row, (128, 128)).T[0:96, 0:1]

    def e_block(ref, chip, rows=slice(None)):
        return ref.at[rows, pl.ds(pl.multiple_of(chip * 384, 128), 384)]

    mine = pl.ds(pl.multiple_of(c * 48, 16), 48)
    other = pl.ds(pl.multiple_of((1 - c) * 48, 16), 48)

    @each(NQ, 0)
    def _(j):
        k = NQ - 1 - j
        pt[...] = dot(rin, e_block(bg, q_of(k))[...])
        keep[k] = pt[mine, :]
        half_s[k] = pt[other, :].astype(BF)
        far(half_s.at[k], half_r.at[k], h_ss.at[k], h_rs.at[k], sib).start()

    @each(NQ)
    def _(j):
        k = NQ - j
        far(half_s.at[k], half_r.at[k], h_ss.at[k], h_rs.at[k], sib).wait_recv()
        rs_s[k] = (keep[k] + half_r[k].astype(F32)).astype(BF)
        far(rs_s.at[k], rs_r.at[k], p_ss.at[k], p_rs.at[k], q_dev(k)).start()

    cols_step(0)

    @each(NY)
    def _(k):
        far(cnt_y.at[y], cnt_y.at[y], n_ss.at[k], n_rs.at[k], y_dev(k)).start()

    far(half_s.at[0], half_r.at[0], h_ss.at[0], h_rs.at[0], sib).wait_recv()
    keep[0] = keep[0] + half_r[0].astype(F32)

    @each(NQ)
    def _(k):
        far(rs_s.at[k], rs_r.at[k], p_ss.at[k], p_rs.at[k], q_dev(k)).wait_recv()
        keep[0] = keep[0] + rs_r[k].astype(F32)

    sg_here = sg[pl.ds(pl.multiple_of(q * 384, 128), 384)].reshape(1, 384)
    denominator = sa_col[mine, :] * sg_here + DAMPING
    sc_own = e_block(sc, q, mine)
    sc_own[...] = (keep[0] / denominator).astype(BF)

    @each(NQ)
    def _(j):
        k = NQ - j
        far(sc_own, sc_own, s_ss.at[k], s_rs.at[k], q_dev(k)).start()

    far(sc_own, sc_own, sf_ss.at[0], sf_rs.at[0], sib).start()

    cols_step(1)
    rows_x.to_core()

    @each(NQ)
    def _(k):
        got = e_block(sc, q_from(k), mine)
        far(got, got, s_ss.at[k], s_rs.at[k], q_dev(k)).wait_recv()
        far(got, got, sf_ss.at[k], sf_rs.at[k], sib).start()

    back[...] = jnp.zeros((192, 96), F32)

    @each(NQ, 0)
    def _(k):
        got = e_block(sc, q_from(k), other)
        far(got, got, sf_ss.at[k], sf_rs.at[k], sib).wait_recv()
        back[...] += dot(e_block(bg, q_from(k))[...], e_block(sc, q_from(k))[...], NT)

    boy_own = y_lanes(boy, y)
    boy_own[:, 0:96] = back[...].astype(BF)
    boy_own[:, 96:128] = jnp.zeros((192, 32), BF)

    @each(NY)
    def _(k):
        far(boy_own, boy_own, o_ss.at[k], o_rs.at[k], y_dev(k)).start()

    cols_step(2)

    @each(NY)
    def _(k):
        slot = y_lanes(boy, y_of(NY - k))
        far(slot, slot, o_ss.at[k], o_rs.at[k], y_dev(k)).wait_recv()

    def pz_half(h, k):
        rows = pl.ds(96 * h, 96)
        return far(pz_s.at[k, rows, :], pz.at[k, rows, :], z_ss.at[h, k], z_rs.at[h, k], z_dev(k))

    @each(NZ + 1)
    def _(j):
        k = jnp.where(j < NZ, opposite_first(j), NZ)
        to = z_of(k)
        rows = r_ba[pl.ds(pl.multiple_of(to * 128, 128), 128), :]
        pz_s[k] = dot(boy[...], rows, NT).astype(BF)

        @pl.when(k < NZ)
        def _():
            pz_half(0, k).start()

    each(NZ)(lambda j: pz_half(1, opposite_first(j)).start())

    rows_x.arrive()

    @each(NY)
    def _(k):
        tile = cnt_y.at[y_of(NY - k)]
        far(tile, tile, n_ss.at[k], n_rs.at[k], y_dev(k)).wait_recv()

    cols_step(3)
    for lo in (0, 256):
        for i in range(NY):
            rows = r_buf[:, i, :, lo : lo + 256].reshape(768, 256)
            term = dot(rows, c_buf[i, :, lo : lo + 256], NT)
            acc[:, lo : lo + 192] = term if i == 0 else acc[:, lo : lo + 192] + term
    cnt_s[...] = cnt_y[0] + cnt_y[1] + cnt_y[2] + cnt_y[3]

    @each(NZ, 0)
    def _(k):
        to = z_of(k)
        rows = pl.ds(pl.multiple_of(to * 96, 32), 96)
        az_s[k] = jnp.concatenate([acc[rows, 0:192], acc[rows, 256:448]], axis=1).astype(BF)

        @pl.when(k > 0)
        def _():
            far(cnt_s, cnt_z.at[k], m_ss.at[k], m_rs.at[k], z_dev(k)).start()

    def sum_rows(way, k):
        return pl.ds(48 * way, 48) if k == 0 else pl.ds(0, 96)

    def sum_copy(way, k):
        rows = sum_rows(way, k)
        return far(az_s.at[(4 - k, 4 + k)[way], rows, :], az.at[way, k, rows, :],
                   a_ss.at[way, k], a_rs.at[way, k], z_dev((1, NZ - 1)[way]))

    def sum_step(k):
        for way in range(2):
            if k > 0:
                sum_copy(way, k - 1).wait_recv()
                rows, at = sum_rows(way, k - 1), (4 - k, 4 + k)[way]
                az_s[at, rows, :] = (az_s[at, rows, :].astype(F32) + az[way, k - 1, rows, :].astype(F32)).astype(BF)
            sum_copy(way, k).start()

    sum_step(0)

    def py_half(h, k):
        slot = py.at[y, pl.ds(96 * h, 96), :]
        return far(slot, slot, q_ss.at[h, k], q_rs.at[h, k], y_dev(k))

    for h in range(2):
        rows = slice(96 * h, 96 * h + 96)
        total = pz_s[NZ, rows, :].astype(F32)
        for k in range(1, NZ):
            pz_half(h, k).wait_recv()
            total = total + pz[k, rows, :].astype(F32)
        py[y, rows, :] = total.astype(BF)
        each(NY)(lambda k: py_half(h, k).start())

    def finish_factors():
        @each(NZ)
        def _(k):
            far(cnt_s, cnt_z.at[k], m_ss.at[k], m_rs.at[k], z_dev(k)).wait_recv()

        for way in range(2):
            sum_copy(way, 3).wait_recv()
        stat = az_s[0].astype(F32) + az[0, 3].astype(F32) + az[1, 3].astype(F32)
        count = cnt_s[...]
        for k in range(1, NZ):
            count = count + cnt_z[k]
        scale = (1.0 - DECAY) / count[0:1, 0:1]
        fa_new[...] = DECAY * fa_old[...] + stat[:, 0:192] * scale
        fg_new[...] = DECAY * fg_old[...] + stat[:, 192:384] * scale

    sum_step(1)

    def ring_copy(h, way, k, arriving):
        at = z_of((NZ - 1, 1)[way] * (k + arriving))
        lo, n = (96 * h, 96) if k < 3 else (96 * h + 48 * way, 48)
        slot = out.at[pl.ds(lo, n), pl.ds(pl.multiple_of(at * 384, 128), 384)]
        return far(slot, slot, f_ss.at[h, way, k], f_rs.at[h, way, k], z_dev((1, NZ - 1)[way]))

    for k in range(5):
        for h in range(2):
            if k == 0:
                rows = pl.ds(96 * h, 96)
                for j in range(1, NY):
                    py_half(h, j).wait_recv()
                out[rows, pl.ds(pl.multiple_of(z * 384, 128), 384)] = lanes4(
                    [py[i, 96 * h : 96 * h + 96, 0:96] for i in range(NY)]
                )
            for way in range(2):
                if k > 0:
                    ring_copy(h, way, k - 1, 1).wait_recv()
                if k < 4:
                    ring_copy(h, way, k, 0).start()
        if k == 0:
            sum_step(2)
        if k == 1:
            sum_step(3)
        if k == 3:
            finish_factors()

    @each(NY)
    def _(k):
        far(y_lanes(rp_s, y), rp_r.at[k], gy_ss.at[k], gy_rs.at[k], y_dev(k)).wait_send()
        far(cnt_y.at[y], cnt_y.at[y], n_ss.at[k], n_rs.at[k], y_dev(k)).wait_send()
        far(boy_own, boy_own, o_ss.at[k], o_rs.at[k], y_dev(k)).wait_send()
        py_half(0, k).wait_send()
        py_half(1, k).wait_send()

    @each(NQ)
    def _(k):
        far(rs_s.at[k], rs_r.at[k], p_ss.at[k], p_rs.at[k], q_dev(k)).wait_send()
        far(sc_own, sc_own, s_ss.at[k], s_rs.at[k], q_dev(k)).wait_send()
        far(g_own, g_own, g_ss.at[k], g_rs.at[k], z_dev(k)).wait_send()
        far(cnt_s, cnt_z.at[k], m_ss.at[k], m_rs.at[k], z_dev(k)).wait_send()
        pz_half(0, k).wait_send()
        pz_half(1, k).wait_send()

    @each(NQ, 0)
    def _(k):
        far(half_s.at[k], half_r.at[k], h_ss.at[k], h_rs.at[k], sib).wait_send()
        far(sc_own, sc_own, sf_ss.at[k], sf_rs.at[k], sib).wait_send()

    for d in range(NY - 1):
        for ok, onward, copy in cols_copies(d):
            pl.when(onward)(copy.wait_send)

    for k in range(4):
        for way in range(2):
            sum_copy(way, k).wait_send()

    rows_b.sent()
    rows_x.sent()

    for h in range(2):
        for way in range(2):
            for k in range(4):
                ring_copy(h, way, k, 0).wait_send()


def local(
    layer_inputs,
    output_cotangents,
    valid,
    factor_a_old,
    factor_g_old,
    weight_gradient,
    basis_g,
    basis_a,
    spectrum_g,
    spectrum_a,
):
    V = pltpu.VMEM
    dma = pltpu.SemaphoreType.DMA
    scratch = [
        V((192, 256), BF), V((192, 256), BF), V((256,), jnp.int32),
        V((96, 192), F32), V((96, 192), F32), V((192, 96), BF),
        V((192, 3072), BF), V((192, 96), BF), V((3072,), F32), V((96,), F32), dma((10,)),
        V((96, 1), F32),
        V((192, 512), BF),
        V((8, 4, 96, 512), BF),
        V((4, 192, 512), BF),
        V((192, 128), BF),
        V((1024, 512), BF),
        V((768, 512), F32),
        V((8, 96, 384), BF),
        V((2, 4, 96, 384), BF),
        V((4, 8, 128), F32),
        V((8, 128), F32),
        V((8, 8, 128), F32),
        V((192, 1024), BF),
        V((192, 512), BF),
        V((4, 192, 128), BF),
        V((96, 384), F32),
        V((8, 48, 384), BF),
        V((8, 48, 384), BF),
        V((8, 48, 384), F32),
        V((8, 48, 384), BF),
        V((8, 48, 384), BF),
        V((96, 3072), BF),
        V((192, 96), F32),
        V((192, 512), BF),
        V((9, 192, 128), BF),
        V((8, 192, 128), BF),
        V((4, 192, 128), BF),
        dma((4,)), dma((4,)),
        dma((8,)), dma((8,)), dma((2, 2, 4)), dma((2, 2, 4)),
        *[dma((4,))] * 6,
        *[dma((4,))] * 6,
        dma((2, 4)), dma((4,)), dma((4,)), dma((4,)), dma((8,)), dma((8,)),
        dma((8,)), dma((8,)), dma((8,)), dma((8,)), dma((8,)), dma((8,)), dma((8,)), dma((8,)),
        dma((2, 4)), dma((2, 4)), dma((4,)), dma((4,)), dma((2, 8)), dma((2, 8)), dma((2, 4)), dma((2, 4)),
    ]
    return pl.pallas_call(
        kernel,
        out_shape=(V((96, 192), F32), V((96, 192), F32), V((192, 3072), BF)),
        in_specs=[pl.BlockSpec(memory_space=pltpu.HBM)] * 10,
        out_specs=(pl.BlockSpec(memory_space=V),) * 3,
        scratch_shapes=scratch,
        compiler_params=pltpu.CompilerParams(
            collective_id=0, has_side_effects=True, vmem_limit_bytes=62 * 1024 * 1024
        ),
    )(
        layer_inputs.T,
        output_cotangents.T,
        valid,
        factor_a_old,
        factor_g_old,
        weight_gradient,
        basis_g,
        basis_a,
        spectrum_g,
        spectrum_a,
    )


def solution(mesh):
    placed = (
        P("rep", "shard"),
        P("rep", "shard"),
        P("rep"),
        P("rep", "shard"),
        P("rep", "shard"),
        P("shard", "rep"),
        P("shard", None),
        P("shard", "rep"),
        P(),
        P("rep"),
    )
    return jax.shard_map(
        local,
        mesh=mesh,
        in_specs=placed,
        out_specs=(P("rep", "shard"), P("rep", "shard"), P("shard", None)),
        check_vma=False,
    )
```
